128 devices in a mesh: lon: 16 (over y, x_lo, core), lat: 8 (over x_hi, z).
Axes of the slice: x: 4 (x_hi: 2, x_lo: 2; x = x_hi * 2 + x_lo), y: 4, z: 4, core: 2. Of those that a mesh axis runs over, the one named last changes fastest.
Arguments:
- tracers: float32 [2, 48, 256, 4096], P(None, None, 'lat', 'lon'), may hold values from -6 to 6
- u_east: float32 [48, 256, 4096], P(None, 'lat', 'lon'), may hold values from -0.15 to 0.15
- v_north: float32 [48, 256, 4096], P(None, 'lat', 'lon'), may hold values from -0.15 to 0.15
- bottom: int32 [256, 4096], P('lat', 'lon'), may hold values from 0 to 48
Outputs:
- advanced: float32 [2, 48, 256, 4096], P(None, None, 'lat', 'lon')
The draws below stay inside these ranges and needn't reach their ends.
All inputs are finite; a program needn't handle non-finite values.
Results may differ from the reference program's by a relative error of at most 0.0003.
Values sent between devices are 32-bit elements; how exact they have to be, the bound alone decides.
No kernel may reach another device: no remote copies, remote signals or barrier semaphores. Data moves between devices by JAX's collectives and lax.ppermute only.
A program may use at most 128 MiB of HBM per device.

```python
import jax
import jax.numpy as jnp

LEV = 48
STEPS = 3
NY = 256
NX = 4096


def plant(values, rng, low, top_value):
    dims = values.shape
    spot = [jax.random.randint(jax.random.fold_in(rng, axis), (), 0, dims[axis]) for axis in range(len(dims))]
    values = values.at[tuple(spot)].set(low)
    longest = dims.index(max(dims))
    spot[longest] = (spot[longest] + 1) % dims[longest]
    return values.at[tuple(spot)].set(top_value)


def shard_levels(stream_key, dims, split, least, high):
    loudness, own = 1.0, jax.random.fold_in(stream_key, 6)
    for position, parts in split:
        draws = jnp.exp(jax.random.uniform(jax.random.fold_in(own, position), (parts,), jnp.float32, least / len(split), high / len(split)))
        loudness = loudness * jnp.repeat(draws, dims[position] // parts).reshape([-1 if axis == position else 1 for axis in range(len(dims))])
    return loudness


def bell_draw(stream_key, extent, deviation, most, shards=(), kind=jnp.bfloat16):
    factor_of = shard_levels(stream_key, extent, shards, -0.22, 0.18) if shards else 1.0
    drawn = jax.random.normal(stream_key, extent, jnp.float32) * deviation * factor_of
    return jnp.minimum(jnp.maximum(drawn, -most), most).astype(kind)


def setup_inputs(seed: int = 0) -> dict:
    seeds = jax.random.split(jax.random.key(seed), 5)
    tracers = bell_draw(seeds[0], (2, LEV, NY, NX), 1.0, 6.0, ((2, 8), (3, 16)), jnp.float32)
    u_east = jnp.clip(jax.random.uniform(seeds[1], (LEV, NY, NX), jnp.float32, -0.15, 0.15) * shard_levels(seeds[1], (LEV, NY, NX), ((1, 8), (2, 16)), -0.4, 0.0), -0.15, 0.15)
    v_north = jnp.clip(jax.random.uniform(seeds[2], (LEV, NY, NX), jnp.float32, -0.15, 0.15) * shard_levels(seeds[2], (LEV, NY, NX), ((1, 8), (2, 16)), -0.4, 0.0), -0.15, 0.15)
    bottom = plant(jax.random.randint(seeds[3], (NY, NX), 0, LEV + 1), jax.random.fold_in(seeds[3], 1), 0, LEV).astype(jnp.int32)
    return {"tracers": tracers, "u_east": u_east, "v_north": v_north, "bottom": bottom}


horiz_kappa = 0.06
vert_kappa = 0.08


def upwind(speed, here, there):
    return 0.5 * (speed + jnp.abs(speed)) * here + 0.5 * (speed - jnp.abs(speed)) * there


def shifted(field, ghost_north):
    east_vals = jnp.roll(field, -1, -1)
    west_vals = jnp.roll(field, 1, -1)
    south_vals = jnp.concatenate([jnp.zeros_like(field[..., :1, :]), field[..., :-1, :]], -2)
    north_vals = jnp.concatenate([field[..., 1:, :], ghost_north[..., None, :]], -2)
    return east_vals, west_vals, south_vals, north_vals


def vertical(field):
    zero_level = jnp.zeros_like(field[..., :1, :, :])
    up_vals = jnp.concatenate([zero_level, field[..., :-1, :, :]], -3)
    down_vals = jnp.concatenate([field[..., 1:, :, :], zero_level], -3)
    return up_vals, down_vals


def tendency(centre, east_vals, west_vals, south_vals, north_vals, u_here, u_west, v_here, v_south, masks):
    mask, mask_e, mask_w, mask_s, mask_n, mask_up, mask_down = masks
    face_e = mask * mask_e
    face_w = mask * mask_w
    face_s = mask * mask_s
    face_n = mask * mask_n
    flux_east = upwind(u_here, centre, east_vals) * face_e
    flux_west = upwind(u_west, west_vals, centre) * face_w
    flux_north = upwind(v_here, centre, north_vals) * face_n
    flux_south = upwind(v_south, south_vals, centre) * face_s
    spread = horiz_kappa * ((east_vals - centre) * face_e + (west_vals - centre) * face_w
                            + (north_vals - centre) * face_n + (south_vals - centre) * face_s)
    up_vals, down_vals = vertical(centre)
    column = vert_kappa * ((up_vals - centre) * mask * mask_up + (down_vals - centre) * mask * mask_down)
    return centre + flux_west - flux_east + flux_south - flux_north + spread + column


def reference(tracers, u_east, v_north, bottom):
    levels = jnp.arange(LEV, dtype=jnp.float32)[:, None, None] + 0.5
    row_index = jnp.arange(NY)[:, None]
    v_open = v_north * (row_index < NY - 1).astype(jnp.float32)
    depth = bottom.astype(jnp.float32)
    depth_e, depth_w, depth_s, depth_n = shifted(depth, depth[NY - 1, ::-1])
    mask = (levels < depth).astype(jnp.float32)
    mask_e = (levels < depth_e).astype(jnp.float32)
    mask_w = (levels < depth_w).astype(jnp.float32)
    mask_s = (levels < depth_s).astype(jnp.float32)
    mask_n = (levels < depth_n).astype(jnp.float32)
    mask_up, mask_down = vertical(mask)
    masks = (mask, mask_e, mask_w, mask_s, mask_n, mask_up, mask_down)
    u_west = jnp.roll(u_east, 1, -1)
    v_south = jnp.concatenate([jnp.zeros_like(v_open[:, :1, :]), v_open[:, :-1, :]], -2)
    state = tracers
    for step_number in range(STEPS):
        east_vals, west_vals, south_vals, north_vals = shifted(state, state[..., NY - 1, ::-1])
        state = tendency(state, east_vals, west_vals, south_vals, north_vals, u_east, u_west, v_open, v_south, masks)
    return state
```

```python
import functools

import jax
import jax.numpy as jnp
from jax import lax
from jax.experimental import pallas as pl
from jax.experimental.pallas import tpu as pltpu
from jax.sharding import PartitionSpec as P

LEV = 48
ROWS = 32
COLS = 256
GHOST = 3
PLANES = ROWS + 2 * GHOST
PAD = 8
DEEP = 64
DROW = 8
ITEMS = 11
SIDE = ITEMS * 2 * LEV
EDGE = SIDE + LEV
PACKED = EDGE + 16
STRIP = 4 * 2 * LEV + ROWS
H_KAPPA = 0.06
V_KAPPA = 0.08
F32 = jnp.float32


def lanes():
    return lax.broadcasted_iota(jnp.int32, (8, 128), 1)


def to_slot(x, slot):
    return pltpu.roll(x, (8 * slot + 3) % 128, 1)


def from_slot(x, slot):
    return pltpu.roll(x, (128 - 8 * slot - 3) % 128, 1)


def dot_exact(a, b):
    return jnp.dot(a, b, preferred_element_type=F32, precision=lax.Precision.HIGHEST)


def load_kernel(tr, u, v, bottom, x, up, vp, dp, strip, nat, sems):
    lat = lax.axis_index("lat")
    top = lat == lax.axis_size("lat") - 1
    sources = [tr.at[0], tr.at[1], u, v]

    def copy(f, half):
        return pltpu.make_async_copy(
            sources[f].at[:, pl.ds(128 * half, 128)], nat.at[f, half], sems.at[f, half]
        )

    for f in range(4):
        for half in range(2):
            copy(f, half).start()

    depth = bottom[...].astype(F32)
    dp[...] = jnp.zeros_like(dp)
    for half in range(2):
        dp[half, pl.ds(DROW, ROWS), :] = depth[:, 128 * half : 128 * half + 128]
    strip_lane = lax.broadcasted_iota(jnp.int32, (ROWS, 128), 1)
    strip[pl.ds(8 * LEV, ROWS), :] = jnp.where(strip_lane < 64, depth[:, :128], depth[:, 128:])

    zeros = jnp.zeros((8, 128), F32)
    lane = lanes()
    for f in range(4):
        copy(f, 0).wait()
        copy(f, 1).wait()

        def turn(r, _, f=f):
            for half in range(2):
                for k in range(LEV // 8):
                    tile = nat[f, half, pl.ds(8 * k * ROWS + r, 8, stride=ROWS), :]
                    if f < 2:
                        x[f, r + GHOST, half, pl.ds(PAD + 8 * k, 8), :] = tile
                    elif f == 2:
                        up[r + GHOST, half, pl.ds(8 * k, 8), :] = tile
                    else:
                        closed = jnp.logical_and(top, r == ROWS - 1)
                        vp[r + GHOST, half, pl.ds(8 * k, 8), :] = jnp.where(closed, 0.0, tile)
            return 0

        lax.fori_loop(0, ROWS, turn, 0)

        def pack(j, _, f=f):
            part = j // 6
            k = j % 6
            total = zeros
            for s in range(16):
                r = part * 16 + s
                if f < 2:
                    a = x[f, r + GHOST, 0, pl.ds(PAD + 8 * k, 8), :]
                    b = x[f, r + GHOST, 1, pl.ds(PAD + 8 * k, 8), :]
                else:
                    ref = up if f == 2 else vp
                    a = ref[r + GHOST, 0, pl.ds(8 * k, 8), :]
                    b = ref[r + GHOST, 1, pl.ds(8 * k, 8), :]
                both = to_slot(jnp.where(lane < 64, a, b), s)
                total = jnp.where(lane // 8 == s, both, total)
            strip[pl.ds((f * 2 + part) * LEV + 8 * k, 8), :] = total
            return 0

        lax.fori_loop(0, 12, pack, 0)

    def clear(i, _):
        for f in range(2):
            for third in range(3):
                x[f, i, third, pl.ds(0, 8), :] = zeros
                x[f, i, third, pl.ds(DEEP - 8, 8), :] = zeros
        return 0

    lax.fori_loop(0, PLANES, clear, 0)


def rows_kernel(from_east, from_west, x_in, up_in, vp_in, dp_in, x, up, vp, dp, first, second):
    lat = lax.axis_index("lat")
    top = lat == lax.axis_size("lat") - 1
    even = lat % 2 == 0
    lane = lanes()
    strip_lane = lax.broadcasted_iota(jnp.int32, (ROWS, 128), 1)
    dp[2, pl.ds(DROW, ROWS), :] = jnp.where(
        strip_lane < 64, from_east[pl.ds(8 * LEV, ROWS), :], from_west[pl.ds(8 * LEV, ROWS), :]
    )

    for f in range(4):

        def unpack(j, _, f=f):
            part = j // 6
            k = j % 6
            at = pl.ds((f * 2 + part) * LEV + 8 * k, 8)
            both = jnp.where(lane % 8 < 3, from_west[at, :], from_east[at, :])
            for s in range(16):
                i = part * 16 + s + GHOST
                tile = from_slot(both, s)
                if f < 2:
                    x[f, i, 2, pl.ds(PAD + 8 * k, 8), :] = tile
                elif f == 2:
                    up[i, 2, pl.ds(8 * k, 8), :] = tile
                else:
                    vp[i, 2, pl.ds(8 * k, 8), :] = tile
            return 0

        lax.fori_loop(0, 12, unpack, 0)

    def fill(out, north):
        def row(i):
            return jnp.where(north, ROWS - 1 - i, i) + GHOST

        def face(j):
            return jnp.where(north, ROWS - 1 - j, max(j - 1, 0)) + GHOST

        items = [(x.at[t], row(i), PAD) for t in range(2) for i in range(3)]
        items += [(vp, face(j), 0) for j in range(3)]
        items += [(up, row(i), 0) for i in range(2)]
        for k in range(LEV // 8):
            total = jnp.zeros((8, 128), F32)
            for n, (ref, i, offset) in enumerate(items):
                for half in range(2):
                    out[pl.ds((2 * n + half) * LEV + 8 * k, 8), :] = ref[
                        i, half, pl.ds(offset + 8 * k, 8), :
                    ]
                third = to_slot(ref[i, 2, pl.ds(offset + 8 * k, 8), :], n)
                total = jnp.where(lane // 8 == n, third, total)
            out[pl.ds(SIDE + 8 * k, 8), :] = total
        out[pl.ds(EDGE, 16), :] = jnp.zeros((16, 128), F32)
        for i in range(3):
            for third in range(3):
                out[pl.ds(EDGE + 3 * i + third, 1), :] = dp[third, pl.ds(row(i) - GHOST + DROW, 1), :]

    fill(first, even)
    fill(second, jnp.logical_not(even))

    @pl.when(top)
    def _():
        a = lax.broadcasted_iota(jnp.int32, (128, 128), 0)
        b = lax.broadcasted_iota(jnp.int32, (128, 128), 1)
        whole = (a + b == 127).astype(F32)
        slots = jnp.logical_and(a // 8 == b // 8, a % 8 + b % 8 == 5).astype(F32)

        def turn(n, _):
            left = second[pl.ds(2 * n * LEV, LEV), :]
            right = second[pl.ds((2 * n + 1) * LEV, LEV), :]
            second[pl.ds(2 * n * LEV, LEV), :] = dot_exact(right, whole)
            second[pl.ds((2 * n + 1) * LEV, LEV), :] = dot_exact(left, whole)
            return 0

        lax.fori_loop(0, ITEMS, turn, 0)
        second[pl.ds(SIDE, LEV), :] = dot_exact(second[pl.ds(SIDE, LEV), :], slots)
        turned = dot_exact(second[pl.ds(EDGE, 16), :], whole)
        for i in range(3):
            for third in range(3):
                source = 3 * i + (1, 0, 2)[third]
                second[pl.ds(EDGE + 3 * i + third, 1), :] = turned[source : source + 1, :]


def east_of(tiles, lane):
    turned = [pltpu.roll(tile, 127, 1) for tile in tiles]
    return [jnp.where(lane == 127, turned[(n + 1) % 3], turned[n]) for n in range(3)]


def west_of(tiles, lane):
    turned = [pltpu.roll(tile, 1, 1) for tile in tiles]
    return [jnp.where(lane == 0, turned[(n + 2) % 3], turned[n]) for n in range(3)]


def depth_row(dp, i):
    return [
        jnp.broadcast_to(dp[n, pl.ds(i - GHOST + DROW, 1), :], (8, 128)) for n in range(3)
    ]


def level_of(k):
    return (lax.broadcasted_iota(jnp.int32, (8, 128), 0) + 8 * k).astype(F32)


def make_faces(i, vp, dp, cr, ct):
    here, north = depth_row(dp, i), depth_row(dp, i + 1)
    for n in range(3):
        least = jnp.minimum(here[n], north[n])
        for k in range(LEV // 8):
            at = pl.ds(8 * k, 8)
            speed = vp[i, n, at, :]
            opened = level_of(k) < least
            cr[i, n, at, :] = jnp.where(opened, jnp.maximum(speed, 0.0) + H_KAPPA, 0.0)
            ct[i, n, at, :] = jnp.where(opened, H_KAPPA - jnp.minimum(speed, 0.0), 0.0)


def make_cells(i, up, dp, cc, ce, cw, cr, ct, ck):
    lane = lanes()
    here = depth_row(dp, i)
    least = [jnp.minimum(a, b) for a, b in zip(here, east_of(here, lane))]
    for k in range(LEV // 8):
        at = pl.ds(8 * k, 8)
        level = level_of(k)
        above = jnp.where(level > 0.0, level, 1e9) if k == 0 else level
        outs, backs = [], []
        for n in range(3):
            speed = up[i, n, at, :]
            opened = level < least[n]
            outs.append(jnp.where(opened, jnp.maximum(speed, 0.0) + H_KAPPA, 0.0))
            backs.append(jnp.where(opened, H_KAPPA - jnp.minimum(speed, 0.0), 0.0))
        from_west, to_west = west_of(outs, lane), west_of(backs, lane)
        for n in range(3):
            down = jnp.where(level + 1.0 < here[n], V_KAPPA, 0.0)
            upward = jnp.where(above < here[n], V_KAPPA, 0.0)
            ce[i, n, at, :] = backs[n]
            cw[i, n, at, :] = from_west[n]
            ck[i, n, pl.ds(PAD + 8 * k, 8), :] = down
            leaving = (outs[n] + to_west[n]) + (cr[i, n, at, :] + ct[i - 1, n, at, :]) + (down + upward)
            cc[i, n, at, :] = 1.0 - leaving


def advance(i, old, cc, ce, cw, cr, ct, ck, put, tiles=3):
    lane = lanes()
    for k in range(LEV // 8):
        at = pl.ds(8 * k, 8)
        here = pl.ds(PAD + 8 * k, 8)
        above = pl.ds(PAD + 8 * k - 1, 8)
        below = pl.ds(PAD + 8 * k + 1, 8)
        centre = [[old[t, i, n, here, :] for n in range(3)] for t in range(2)]
        east = [east_of(c, lane) for c in centre]
        west = [west_of(c, lane) for c in centre]
        for n in range(tiles):
            c_c, c_e, c_w = cc[i, n, at, :], ce[i, n, at, :], cw[i, n, at, :]
            c_n, c_s = ct[i, n, at, :], cr[i - 1, n, at, :]
            c_d, c_u = ck[i, n, here, :], ck[i, n, above, :]
            for t in range(2):
                total = c_c * centre[t][n] + c_e * east[t][n] + c_w * west[t][n]
                total += c_n * old[t, i + 1, n, here, :] + c_s * old[t, i - 1, n, here, :]
                total += c_u * old[t, i, n, above, :] + c_d * old[t, i, n, below, :]
                put(t, n, k, total)


def put_plane(new, i):
    def put(t, n, k, value):
        new[t, i, n, pl.ds(PAD + 8 * k, 8), :] = value

    return put


def put_rows(out, i):
    def put(t, n, k, value):
        out[t, n, pl.ds(8 * k * ROWS + i - GHOST, 8, stride=ROWS), :] = value

    return put


def inner_kernel(x_in, up, vp, dp, x, y, cc, ce, cw, cr, ct, ck, out):
    coefs = (cc, ce, cw, cr, ct, ck)
    zeros = jnp.zeros((8, 128), F32)

    def clear(i, _):
        for n in range(3):
            ck[i, n, pl.ds(0, 8), :] = zeros
            for t in range(2):
                y[t, i, n, pl.ds(0, 8), :] = zeros
                y[t, i, n, pl.ds(DEEP - 8, 8), :] = zeros
        return 0

    lax.fori_loop(0, PLANES, clear, 0)
    low, high = GHOST, GHOST + ROWS

    def setup(i, _):
        make_faces(i, vp, dp, cr, ct)
        make_cells(i, up, dp, *coefs)
        return 0

    lax.fori_loop(low, high - 1, setup, 0)

    def one(i, _):
        advance(i, x, *coefs, put_plane(y, i))
        return 0

    lax.fori_loop(low + 1, high - 1, one, 0)

    def two(i, _):
        advance(i, y, *coefs, put_plane(x, i))
        return 0

    lax.fori_loop(low + 2, high - 2, two, 0)

    def three(i, _):
        advance(i, x, *coefs, put_rows(out, i), 2)
        return 0

    lax.fori_loop(low + 3, high - 3, three, 0)


def rim_kernel(
    got_first, got_second, x_in, y_in, cc_in, ce_in, cw_in, cr_in, ct_in, ck_in, rows_in, up_in, vp_in, dp_in,
    result, x, y, cc, ce, cw, cr, ct, ck, rows, up, vp, dp, sems,
):
    lat = lax.axis_index("lat")
    top = lat == lax.axis_size("lat") - 1
    even = lat % 2 == 0
    lane = lanes()
    coefs = (cc, ce, cw, cr, ct, ck)

    def unpack(got, north, mirrored):
        def plane(i):
            return GHOST + ROWS + i if north else GHOST - 1 - i

        places = [(x.at[t], plane(i), PAD) for t in range(2) for i in range(3)]
        places += [(vp, plane(j - 1 if north else j), 0) for j in range(3)]
        places += [(up, plane(i), 0) for i in range(2)]
        for n, (ref, i, offset) in enumerate(places):
            if north and n == 6:
                continue
            for k in range(LEV // 8):
                at = pl.ds(offset + 8 * k, 8)
                tiles = [got[pl.ds((2 * n + half) * LEV + 8 * k, 8), :] for half in range(2)]
                tiles.append(from_slot(got[pl.ds(SIDE + 8 * k, 8), :], n))
                if north and 6 <= n < 9:
                    tiles = [jnp.where(mirrored, -tile, tile) for tile in tiles]
                if north and n >= 9:
                    shifted = east_of(tiles, lane)
                    tiles = [jnp.where(mirrored, -b, a) for a, b in zip(tiles, shifted)]
                for third in range(3):
                    ref[i, third, at, :] = tiles[third]
        for i in range(3):
            for third in range(3):
                dp[third, pl.ds(plane(i) - GHOST + DROW, 1), :] = got[pl.ds(EDGE + 3 * i + third, 1), :]

    @pl.when(even)
    def _():
        unpack(got_first, True, False)
        unpack(got_second, False, False)

    @pl.when(jnp.logical_not(even))
    def _():
        unpack(got_second, True, top)
        unpack(got_first, False, False)

    south, north = GHOST, GHOST + ROWS

    def rim(count, body):
        def step(j, _):
            body(j)
            return 0

        lax.fori_loop(0, count, step, 0)

    rim(3, lambda j: make_faces(south - 3 + j, vp, dp, cr, ct))
    rim(3, lambda j: make_faces(north - 1 + j, vp, dp, cr, ct))
    rim(3, lambda j: make_cells(south - 2 + j, up, dp, *coefs))
    rim(3, lambda j: make_cells(north - 1 + j, up, dp, *coefs))

    def both(shift, old, put):
        def body(j):
            i = jnp.where(j < 3, south - shift + j, north + shift - 3 + j - 3)
            advance(i, old, *coefs, put(i), 2 if shift == 0 else 3)

        rim(6, body)

    both(2, x, functools.partial(put_plane, y))
    both(1, y, functools.partial(put_plane, x))
    both(0, x, functools.partial(put_rows, rows))
    copies = [
        pltpu.make_async_copy(
            rows.at[t, half], result.at[t, :, pl.ds(128 * half, 128)], sems.at[t, half]
        )
        for t in range(2)
        for half in range(2)
    ]
    for one in copies:
        one.start()
    for one in copies:
        one.wait()


def vmem(shape):
    return pltpu.VMEM(shape, F32)


def here(array):
    return pltpu.with_memory_space_constraint(array, pltpu.VMEM)


def far(array):
    return pltpu.with_memory_space_constraint(array, pltpu.HBM)


IN_VMEM = pl.BlockSpec(memory_space=pltpu.VMEM)
ANYWHERE = pl.BlockSpec(memory_space=pl.ANY)
STATE = (2, PLANES, 3, DEEP, 128)
COEF = (PLANES, 3, LEV, 128)
COLUMN = (PLANES, 3, DEEP, 128)
DEPTH = (3, DROW + ROWS + 8, 128)
NATURAL = (2, 2, LEV * ROWS, 128)


def call(kernel, args, outs, aliases=None, limit=4, **more):
    return pl.pallas_call(
        kernel,
        out_shape=outs,
        input_output_aliases=aliases or {},
        compiler_params=pltpu.CompilerParams(vmem_limit_bytes=limit << 20),
        **more,
    )(*args)


def local(tracers, u_east, v_north, bottom):
    lon_size, lat_size = lax.axis_size("lon"), lax.axis_size("lat")
    flat = LEV * ROWS
    x, up, vp, dp, strip = call(
        load_kernel,
        (
            far(tracers.reshape(2, flat, COLS)),
            far(u_east.reshape(flat, COLS)),
            far(v_north.reshape(flat, COLS)),
            far(bottom),
        ),
        [vmem(STATE), vmem(COEF), vmem(COEF), vmem(DEPTH), jax.ShapeDtypeStruct((STRIP, 128), F32)],
        in_specs=[pl.BlockSpec(memory_space=pltpu.HBM)] * 3 + [IN_VMEM],
        out_specs=[IN_VMEM] * 5,
        scratch_shapes=[pltpu.VMEM((4, 2, flat, 128), F32), pltpu.SemaphoreType.DMA((4, 2))],
        limit=12,
        name="load",
    )
    eastward = [(i, (i + 1) % lon_size) for i in range(lon_size)]
    from_west = lax.ppermute(strip, "lon", eastward)
    from_east = lax.ppermute(strip, "lon", [(b, a) for a, b in eastward])

    payload = jax.ShapeDtypeStruct((PACKED, 128), F32)
    x, up, vp, dp, first, second = call(
        rows_kernel,
        (from_east, from_west, here(x), here(up), here(vp), here(dp)),
        [vmem(STATE), vmem(COEF), vmem(COEF), vmem(DEPTH), payload, payload],
        {2: 0, 3: 1, 4: 2, 5: 3},
        in_specs=[IN_VMEM] * 6,
        out_specs=[IN_VMEM] * 6,
        name="rows",
    )
    got_first = lax.ppermute(first, "lat", [(a, a ^ 1) for a in range(lat_size)])
    pairs = []
    for lon in range(lon_size):
        for lat in range(1, lat_size - 1):
            pairs.append((lon * lat_size + lat, lon * lat_size + (lat + 1 if lat % 2 else lat - 1)))
        pairs.append((lon * lat_size + lat_size - 1, (lon_size - 1 - lon) * lat_size + lat_size - 1))
    got_second = lax.ppermute(second, ("lon", "lat"), pairs)

    x, y, *coefs, rows = call(
        inner_kernel,
        (here(x), here(up), here(vp), here(dp)),
        [vmem(STATE), vmem(STATE)] + [vmem(COEF)] * 5 + [vmem(COLUMN), vmem(NATURAL)],
        {0: 0},
        in_specs=[IN_VMEM] * 4,
        out_specs=[IN_VMEM] * 9,
        name="inner",
        cost_estimate=pl.CostEstimate(flops=60_000_000, bytes_accessed=20_000_000, transcendentals=0),
    )
    held = [x, y, *coefs, rows, up, vp, dp]
    result = call(
        rim_kernel,
        (got_first, got_second, *[here(a) for a in held]),
        [jax.ShapeDtypeStruct((2, flat, COLS), F32)]
        + [vmem(s) for s in [STATE, STATE] + [COEF] * 5 + [COLUMN, NATURAL, COEF, COEF, DEPTH]],
        {2 + n: 1 + n for n in range(12)},
        in_specs=[IN_VMEM] * 14,
        out_specs=[ANYWHERE] + [IN_VMEM] * 12,
        scratch_shapes=[pltpu.SemaphoreType.DMA((2, 2))],
        name="rim",
    )[0]
    return result.reshape(tracers.shape)


def solution(mesh):
    placed = (
        P(None, None, "lat", "lon"),
        P(None, "lat", "lon"),
        P(None, "lat", "lon"),
        P("lat", "lon"),
    )
    return jax.shard_map(
        local, mesh=mesh, in_specs=placed, out_specs=P(None, None, "lat", "lon"), check_vma=False
    )
```

```python
import functools

import jax
import jax.numpy as jnp
from jax import lax
from jax.experimental import pallas as pl
from jax.experimental.pallas import tpu as pltpu
from jax.sharding import PartitionSpec as P

LEV = 48
BANDS = LEV // 8
ROWS = 32
COLS = 256
GHOST = 3
PLANES = ROWS + 2 * GHOST
PAD = 8
DEEP = 64
DROW = 8
ITEMS = 11
DEPTHS = ITEMS * 2 * LEV
CORNERS = DEPTHS + 16
CORNER = LEV + 16
PACKED = CORNERS + CORNER
STRIP = 4 * 2 * LEV + ROWS
H_KAPPA = 0.06
V_KAPPA = 0.08
SHUT = 1e30
F32 = jnp.float32


def lanes():
    return lax.broadcasted_iota(jnp.int32, (8, 128), 1)


def turned(x, shift):
    return pltpu.roll(x, shift % 128 if isinstance(shift, int) else lax.rem(shift + 1024, 128), 1)


def gathered(x, index):
    return jnp.take_along_axis(x, index, axis=1)


def is_top():
    return lax.axis_index("lat") == lax.axis_size("lat") - 1


def is_even():
    return lax.axis_index("lat") % 2 == 0


def rows_kernel(x, up, vp, dp, first, second, sems):
    even = is_even()

    def fill(out, north, sem):
        def row(i):
            return jnp.where(north, ROWS - 1 - i, i) + GHOST

        def face(j):
            return jnp.where(north, ROWS - 1 - j, max(j - 1, 0)) + GHOST

        items = [(x.at[t], row(i), PAD) for t in range(2) for i in range(3)]
        items += [(vp, face(j), 0) for j in range(3)] + [(up, row(i), 0) for i in range(2)]
        for n, (ref, i, offset) in enumerate(items):
            for half in range(2):
                pltpu.make_async_copy(
                    ref.at[i, half, pl.ds(offset, LEV), :],
                    out.at[pl.ds((2 * n + half) * LEV, LEV), :],
                    sem,
                ).start()

    def finish(out, north, sem):
        all_items = out.at[pl.ds(0, DEPTHS), :]
        pltpu.make_async_copy(all_items, all_items, sem).wait()
        out[pl.ds(DEPTHS, 16), :] = jnp.zeros((16, 128), F32)
        for i in range(3):
            r = jnp.where(north, ROWS - 1 - i, i)
            for half in range(2):
                out[pl.ds(DEPTHS + 2 * i + half, 1), :] = dp[half, pl.ds(r + DROW, 1), :]

    odd = jnp.logical_not(even)
    fill(first, even, sems.at[0])
    fill(second, odd, sems.at[1])
    finish(first, even, sems.at[0])
    finish(second, odd, sems.at[1])

    @pl.when(is_top())
    def _():
        back = 127 - lanes()

        def turn(n, _):
            for k in range(BANDS):
                a = pl.ds(2 * n * LEV + 8 * k, 8)
                b = pl.ds((2 * n + 1) * LEV + 8 * k, 8)
                left, right = second[a, :], second[b, :]
                second[a, :] = gathered(right, back)
                second[b, :] = gathered(left, back)
            return 0

        lax.fori_loop(0, ITEMS, turn, 0)
        rows = gathered(second[pl.ds(DEPTHS, 8), :], back)
        for i in range(3):
            for half in range(2):
                source = 2 * i + 1 - half
                second[pl.ds(DEPTHS + 2 * i + half, 1), :] = rows[source : source + 1, :]


def load_kernel(tr, u, v, bottom, x, up, vp, dp, strip, sems):
    def start(r, _):
        for half in range(2):
            columns = pl.ds(128 * half, 128)
            pltpu.make_async_copy(
                tr.at[:, :, r, columns], x.at[:, r + GHOST, half, pl.ds(PAD, LEV), :], sems.at[0]
            ).start()
        return 0

    def start_flow(r, _, source=None, into=None, sem=None):
        for half in range(2):
            pltpu.make_async_copy(
                source.at[:, r, pl.ds(128 * half, 128)], into.at[r + GHOST, half], sem
            ).start()
        return 0

    lax.fori_loop(0, ROWS, functools.partial(start_flow, source=u, into=up, sem=sems.at[1]), 0)
    lax.fori_loop(0, ROWS, functools.partial(start_flow, source=v, into=vp, sem=sems.at[2]), 0)
    lax.fori_loop(0, ROWS, start, 0)

    depth = bottom[...].astype(F32)
    dp[...] = jnp.zeros_like(dp)
    for half in range(2):
        dp[half, pl.ds(DROW, ROWS), :] = depth[:, 128 * half : 128 * half + 128]
    strip_lane = lax.broadcasted_iota(jnp.int32, (ROWS, 128), 1)
    strip[pl.ds(8 * LEV, ROWS), :] = jnp.where(strip_lane < 64, depth[:, :128], depth[:, 128:])

    zeros = jnp.zeros((8, 128), F32)
    lane = lanes()

    def clear(i, _):
        for t in range(2):
            for half in range(2):
                x[t, i, half, pl.ds(0, 8), :] = zeros
                x[t, i, half, pl.ds(DEEP - 8, 8), :] = zeros
        return 0

    lax.fori_loop(0, PLANES, clear, 0)

    def pack(f, load):
        def one(k, _):
            for part in range(2):
                total = zeros
                for s in range(16):
                    a, b = load(part * 16 + s + GHOST, k)
                    both = turned(jnp.where(lane < 64, a, b), 8 * s + 3)
                    total = jnp.where(lane // 8 == s, both, total)
                strip[pl.ds((f * 2 + part) * LEV + 8 * k, 8), :] = total
            return 0

        lax.fori_loop(0, BANDS, one, 0)

    own = pl.ds(GHOST, ROWS)
    for n, ref in ((1, up), (2, vp)):
        pltpu.make_async_copy(ref.at[own], ref.at[own], sems.at[n]).wait()
        if n == 2:

            @pl.when(is_top())
            def _():
                for half in range(2):
                    vp[GHOST + ROWS - 1, half] = jnp.zeros((LEV, 128), F32)

        pack(n + 1, lambda i, k, ref=ref: [ref[i, half, pl.ds(8 * k, 8), :] for half in range(2)])
    whole = x.at[:, own, :, pl.ds(PAD, LEV), :]
    pltpu.make_async_copy(whole, whole, sems.at[0]).wait()
    for t in range(2):
        pack(t, lambda i, k, t=t: [x[t, i, half, pl.ds(PAD + 8 * k, 8), :] for half in range(2)])


def level_of(k):
    return (lax.broadcasted_iota(jnp.int32, (8, 128), 0) + 8 * k).astype(F32)


def above_of(k):
    level = level_of(k)
    return jnp.where(level > 0.0, level, 1e9) if k == 0 else level


def forth(speed, opened):
    return jnp.where(opened, jnp.maximum(speed, 0.0) + H_KAPPA, 0.0)


def back(speed, opened):
    return jnp.where(opened, H_KAPPA - jnp.minimum(speed, 0.0), 0.0)


def depth_row(dp, i, count):
    at = pl.ds(i - GHOST + DROW, 1)
    return [jnp.broadcast_to(dp[n, at, :], (8, 128)) for n in range(count)]


def make_faces(i, vp, dp, cr, ct):
    here, north = depth_row(dp, i, 2), depth_row(dp, i + 1, 2)
    for n in range(2):
        least = jnp.minimum(here[n], north[n])
        for k in range(BANDS):
            at = pl.ds(8 * k, 8)
            speed = vp[i, n, at, :]
            opened = level_of(k) < least
            cr[i, n, at, :] = forth(speed, opened)
            ct[i, n, at, :] = back(speed, opened)


def make_column(i, dp, ck):
    here = depth_row(dp, i, 2)
    for n in range(2):
        ck[i, n, pl.ds(0, 8), :] = jnp.zeros((8, 128), F32)
        for k in range(BANDS):
            ck[i, n, pl.ds(PAD + 8 * k, 8), :] = jnp.where(level_of(k) + 1.0 < here[n], V_KAPPA, 0.0)


def make_cells(rows, up, dp, edge_speed, cc, ce, cw, cr, ct, ck):
    lane = lanes()
    leasts = []
    for i, _, _ in rows:
        here = depth_row(dp, i, 3)
        east = [turned(h, -1) for h in here]
        leasts.append([jnp.minimum(here[n], jnp.where(lane == 127, east[n + 1], east[n])) for n in range(2)])
    for k in range(BANDS):
        at = pl.ds(8 * k, 8)
        for (i, part, slot), least in zip(rows, leasts):
            speeds = [jnp.where(level_of(k) < least[n], up[i, n, at, :], SHUT) for n in range(2)]
            a, b = [turned(speed, 1) for speed in speeds]
            outer = turned(edge_speed[part, at, :], -8 * slot - 2)
            wests = [jnp.where(lane == 0, outer, a), jnp.where(lane == 0, a, b)]
            for n in range(2):
                open_e, open_w = speeds[n] < SHUT, wests[n] < SHUT
                to_east = forth(speeds[n], open_e)
                from_east = back(speeds[n], open_e)
                ce[i, n, at, :] = from_east
                cw[i, n, at, :] = forth(wests[n], open_w)
                column = ck[i, n, pl.ds(PAD + 8 * k, 8), :] + ck[i, n, pl.ds(PAD + 8 * k - 1, 8), :]
                flows = (to_east + back(wests[n], open_w)) + (cr[i, n, at, :] + ct[i - 1, n, at, :])
                cc[i, n, at, :] = 1.0 - (flows + column)


def next_slot(tiles, lane):
    moved = [turned(t, -8) for t in tiles]
    return [jnp.where(lane >= 120, moved[(p + 1) % len(tiles)], moved[p]) for p in range(len(tiles))]


def last_slot(tiles, lane):
    moved = [turned(t, 8) for t in tiles]
    return [jnp.where(lane < 8, moved[p - 1], moved[p]) for p in range(len(tiles))]


def edge_depths(dp, side, rows):
    lane = lanes()
    tiles = []
    for part in range(len(rows) // 16):
        total = jnp.zeros((8, 128), F32)
        for s in range(16):
            near, beyond = depth_row(dp, rows[part * 16 + s] + GHOST, 3)[side], None
            beyond = depth_row(dp, rows[part * 16 + s] + GHOST, 3)[2]
            both = jnp.where(lane < 64, near, beyond) if side == 0 else jnp.where(lane < 64, beyond, near)
            total = jnp.where(lane // 8 == s, turned(both, 8 * s + 3), total)
        tiles.append(total)
    return tiles


def edge_coefs(side, parts, depths, eu, ev, ecoef, eck, edge_speed):
    lane = lanes()
    depth_e = [turned(d, -1) for d in depths]
    depth_n = next_slot(depths, lane)
    every = range(parts)
    for k in range(BANDS):
        at = pl.ds(8 * k, 8)
        level = level_of(k)
        us = [eu[side, p, at, :] for p in every]
        vs = [ev[side, p, at, :] for p in every]
        open_e = [level < jnp.minimum(depths[p], depth_e[p]) for p in every]
        open_n = [level < jnp.minimum(depths[p], depth_n[p]) for p in every]
        outs = [forth(us[p], open_e[p]) for p in every]
        backs = [back(us[p], open_e[p]) for p in every]
        norths = [forth(vs[p], open_n[p]) for p in every]
        souths = [back(vs[p], open_n[p]) for p in every]
        from_south, to_south = last_slot(norths, lane), last_slot(souths, lane)
        for p in every:
            down = jnp.where(level + 1.0 < depths[p], V_KAPPA, 0.0)
            upward = jnp.where(above_of(k) < depths[p], V_KAPPA, 0.0)
            flows = (outs[p] + turned(backs[p], 1)) + (norths[p] + to_south[p])
            ecoef[side, p, 0, at, :] = 1.0 - (flows + (down + upward))
            ecoef[side, p, 1, at, :] = backs[p]
            ecoef[side, p, 2, at, :] = turned(outs[p], 1)
            ecoef[side, p, 3, at, :] = souths[p]
            ecoef[side, p, 4, at, :] = from_south[p]
            eck[side, p, pl.ds(PAD + 8 * k, 8), :] = down
            if k == 0:
                eck[side, p, pl.ds(0, 8), :] = jnp.zeros((8, 128), F32)
            if side == 0:
                edge_speed[p, at, :] = jnp.where(open_e[p], us[p], SHUT)


def edge_step(parts, old, new, ecoef, eck):
    lane = lanes()

    def one(j, _):
        t = j // 2
        side = j % 2
        for k in range(BANDS):
            at = pl.ds(8 * k, 8)
            here = pl.ds(PAD + 8 * k, 8)
            above = pl.ds(PAD + 8 * k - 1, 8)
            below = pl.ds(PAD + 8 * k + 1, 8)
            tiles = [old[t, side, p, here, :] for p in range(parts)]
            north, south = next_slot(tiles, lane), last_slot(tiles, lane)
            for p in range(parts):
                c = [ecoef[side, p, n, at, :] for n in range(5)]
                total = c[0] * tiles[p] + c[1] * turned(tiles[p], -1) + c[2] * turned(tiles[p], 1)
                total += c[3] * north[p] + c[4] * south[p]
                total += eck[side, p, above, :] * old[t, side, p, above, :]
                total += eck[side, p, here, :] * old[t, side, p, below, :]
                new[t, side, p, here, :] = total
        return 0

    lax.fori_loop(0, 4, one, 0)


def edge_beside(parts, old, beside):
    lane = lanes()
    for t in range(2):
        for p in range(parts):
            for k in range(BANDS):
                here = pl.ds(PAD + 8 * k, 8)
                west, east = old[t, 0, p, here, :], old[t, 1, p, here, :]
                beside[t, p, pl.ds(8 * k, 8), :] = jnp.where(lane % 8 == 3, east, turned(west, 2))


def clear_levels(ref):
    zeros = jnp.zeros((8, 128), F32)
    for t in range(2):
        for side in range(2):
            for p in range(ref.shape[2]):
                ref[t, side, p, pl.ds(0, 8), :] = zeros
                ref[t, side, p, pl.ds(DEEP - 8, 8), :] = zeros


def faces_kernel(vp, dp, cr, ct, ck):
    def one(i, _):
        make_faces(i, vp, dp, cr, ct)
        make_column(i, dp, ck)
        return 0

    lax.fori_loop(GHOST, GHOST + ROWS, one, 0)


def corner_kernel(from_east, from_west, strip, dp_in, first_in, second_in, pe, dp, first, second):
    lane = lanes()
    strip_lane = lax.broadcasted_iota(jnp.int32, (ROWS, 128), 1)
    edge = pl.ds(8 * LEV, ROWS)
    dp[2, pl.ds(DROW, ROWS), :] = jnp.where(strip_lane < 64, from_east[edge, :], from_west[edge, :])
    for f in range(4):
        for part in range(2):
            for k in range(BANDS):
                at = pl.ds((f * 2 + part) * LEV + 8 * k, 8)
                mine = strip[at, :]
                pe[f, 0, part, pl.ds(8 * k, 8), :] = jnp.where(lane % 8 < 3, from_west[at, :], mine)
                pe[f, 1, part, pl.ds(8 * k, 8), :] = jnp.where(lane % 8 < 3, mine, from_east[at, :])

    def fill(out, north):
        part = jnp.where(north, 1, 0)
        for k in range(BANDS):
            total = jnp.zeros((8, 128), F32)
            for f in range(4):
                for side in range(2):
                    tile = pe[f, side, part, pl.ds(8 * k, 8), :]
                    for g in range(2):
                        n = f * 4 + side * 2 + g
                        moved = turned(tile, 8 * jnp.where(north, n - 15 + g, n - g))
                        total = jnp.where(lane // 8 == n, moved, total)
            out[pl.ds(CORNERS + 8 * k, 8), :] = total
        out[pl.ds(CORNERS + LEV, 16), :] = jnp.zeros((16, 128), F32)
        for i in range(3):
            r = jnp.where(north, ROWS - 1 - i, i)
            out[pl.ds(CORNERS + LEV + i, 1), :] = dp[2, pl.ds(r + DROW, 1), :]

    fill(first, is_even())
    fill(second, jnp.logical_not(is_even()))

    @pl.when(is_top())
    def _():
        place = lane % 8
        source = jnp.where(lane >= 96, (lane // 8 ^ 2) | 1, lane // 8 ^ 2)
        index = 8 * source + jnp.where(place < 6, 5 - place, place)
        for k in range(BANDS):
            at = pl.ds(CORNERS + 8 * k, 8)
            second[at, :] = gathered(second[at, :], index)
        at = pl.ds(CORNERS + LEV, 8)
        second[at, :] = gathered(second[at, :], 127 - lane)


def shift_row(row, k, old, beside, shifted):
    i, part, slot = row
    lane = lanes()
    here = pl.ds(PAD + 8 * k, 8)
    at = pl.ds(8 * k, 8)
    for t in range(2):
        left, right = old[t, i, 0, here, :], old[t, i, 1, here, :]
        outer = turned(beside[t, part, at, :], -8 * slot - 4)
        left_e, right_e = turned(left, -1), turned(right, -1)
        left_w, right_w = turned(left, 1), turned(right, 1)
        shifted[t, 0, at, :] = jnp.where(lane == 127, right_e, left_e)
        shifted[t, 1, at, :] = jnp.where(lane == 127, outer, right_e)
        shifted[t, 2, at, :] = jnp.where(lane == 0, outer, left_w)
        shifted[t, 3, at, :] = jnp.where(lane == 0, left_w, right_w)


def advance_row(i, k, old, new, shifted, cc, ce, cw, cr, ct, ck):
    at = pl.ds(8 * k, 8)
    here = pl.ds(PAD + 8 * k, 8)
    above = pl.ds(PAD + 8 * k - 1, 8)
    below = pl.ds(PAD + 8 * k + 1, 8)
    for n in range(2):
        c_c, c_e, c_w = cc[i, n, at, :], ce[i, n, at, :], cw[i, n, at, :]
        c_n, c_s = ct[i, n, at, :], cr[i - 1, n, at, :]
        c_d, c_u = ck[i, n, here, :], ck[i, n, above, :]
        for t in range(2):
            total = c_c * old[t, i, n, here, :]
            total += c_e * shifted[t, n, at, :] + c_w * shifted[t, 2 + n, at, :]
            total += c_n * old[t, i + 1, n, here, :] + c_s * old[t, i - 1, n, here, :]
            total += c_u * old[t, i, n, above, :] + c_d * old[t, i, n, below, :]
            new[t, i, n, here, :] = total


def send_rows(rows, new, result, sem):
    for i in rows:
        for half in range(2):
            pltpu.make_async_copy(
                new.at[:, i, half, pl.ds(PAD, LEV), :],
                result.at[:, :, i - GHOST, pl.ds(128 * half, 128)],
                sem,
            ).start()


def inner_kernel(
    x_in, up, dp, cr, ct, ck, pe,
    x, y, cc, ce, cw, result, shifted, e0, e1, ecoef, eck, edge_speed, beside, sem,
):
    coefs = (cc, ce, cw, cr, ct, ck)
    zeros = jnp.zeros((8, 128), F32)

    def clear(i, _):
        for t in range(2):
            for n in range(2):
                y[t, i, n, pl.ds(0, 8), :] = zeros
                y[t, i, n, pl.ds(DEEP - 8, 8), :] = zeros
        return 0

    lax.fori_loop(0, PLANES, clear, 0)

    rows = list(range(ROWS))
    clear_levels(e0)
    clear_levels(e1)
    for side in range(2):
        edge_coefs(side, 2, edge_depths(dp, side, rows), pe.at[2], pe.at[3], ecoef, eck, edge_speed)
        for t in range(2):
            for p in range(2):
                e0[t, side, p, pl.ds(PAD, LEV), :] = pe[t, side, p]

    def setup(i, _):
        planes = [GHOST + 1 + 2 * i + n for n in range(2)]
        placed = [(p, (p - GHOST) // 16, (p - GHOST) % 16) for p in planes]
        make_cells(placed, up, dp, edge_speed, *coefs)
        return 0

    lax.fori_loop(0, ROWS // 2 - 1, setup, 0)
    edge_beside(2, e0, beside.at[0])
    edge_step(2, e0, e1, ecoef, eck)
    edge_beside(2, e1, beside.at[1])
    edge_step(2, e1, e0, ecoef, eck)
    edge_beside(2, e0, beside.at[2])

    for step in range(3):
        old, new = (x, y) if step != 1 else (y, x)
        low = GHOST + 1 + step

        def placed(i):
            i = jnp.minimum(i, GHOST + ROWS - 1)
            return i, (i - GHOST) // 16, (i - GHOST) % 16

        for k in range(BANDS):
            shift_row(placed(low), k, old, beside.at[step], shifted.at[0])

        def body(j, _, low=low, old=old, new=new, step=step, placed=placed):
            i = low + 2 * j
            for n in range(2):
                for k in range(BANDS):
                    shift_row(placed(i + n + 1), k, old, beside.at[step], shifted.at[1 - n])
                    advance_row(i + n, k, old, new, shifted.at[n], *coefs)
            if step == 2:
                send_rows([i, i + 1], new, result, sem)
            return 0

        lax.fori_loop(0, (ROWS - 2 - 2 * step) // 2, body, 0)
    sent = y.at[:, pl.ds(2 * GHOST, ROWS - 2 * GHOST), :, pl.ds(PAD, LEV), :]
    pltpu.make_async_copy(sent, sent, sem).wait()


RIM_SOUTH = list(range(-GHOST, 5))
RIM_NORTH = list(range(ROWS - 5, ROWS + GHOST))


def rim_kernel(
    got_first, got_second,
    x_in, y_in, cc_in, ce_in, cw_in, cr_in, ct_in, ck_in, up_in, vp_in, dp_in, pe, result_in,
    x, y, cc, ce, cw, cr, ct, ck, up, vp, dp, result,
    shifted, e0, e1, eflow, ecoef, eck, edge_speed, beside, corners, sem,
):
    lane = lanes()
    coefs = (cc, ce, cw, cr, ct, ck)
    bottommost = lax.axis_index("lat") == 0

    def unpack(got, north, mirrored):
        corner = got.at[pl.ds(CORNERS, CORNER), :]

        def plane(i):
            return GHOST + ROWS + i if north else GHOST - 1 - i

        places = [(x.at[t], plane(i), PAD) for t in range(2) for i in range(3)]
        places += [(vp, plane(j - 1 if north else j), 0) for j in range(3)]
        places += [(up, plane(i), 0) for i in range(2)]
        for n, (ref, i, offset) in enumerate(places):
            if north and n == 6:
                continue
            for k in range(BANDS):
                at = pl.ds(offset + 8 * k, 8)
                tiles = [got[pl.ds((2 * n + half) * LEV + 8 * k, 8), :] for half in range(2)]
                if north and 6 <= n < 9:
                    tiles = [jnp.where(mirrored, -tile, tile) for tile in tiles]
                if north and n >= 9:
                    g = n - 9
                    beyond = turned(corner[pl.ds(8 * k, 8), :], -8 * (2 * 4 + 2 + g) - 3)
                    moved = [turned(tile, -1) for tile in tiles]
                    east = [
                        jnp.where(lane == 127, moved[1], moved[0]),
                        jnp.where(lane == 127, turned(beyond, -1), moved[1]),
                    ]
                    tiles = [jnp.where(mirrored, -b, a) for a, b in zip(tiles, east)]
                for half in range(2):
                    ref[i, half, at, :] = tiles[half]
        for i in range(3):
            at = pl.ds(plane(i) - GHOST + DROW, 1)
            rows = [got[pl.ds(DEPTHS + 2 * i + half, 1), :] for half in range(2)]
            rows.append(corner[pl.ds(LEV + i, 1), :])
            for third in range(3):
                dp[third, at, :] = rows[third] if north else jnp.where(bottommost, 0.0, rows[third])
        for k in range(BANDS):
            at = pl.ds(8 * k, 8)
            tile = corner[at, :]
            if north:
                west_face = -turned(tile, -1)
                changed = jnp.where(lane >= 96, -tile, jnp.where(lane >= 64, west_face, tile))
                tile = jnp.where(mirrored, changed, tile)
            corners[1 if north else 0, at, :] = tile

    @pl.when(is_even())
    def _():
        unpack(got_first, True, False)
        unpack(got_second, False, False)

    @pl.when(jnp.logical_not(is_even()))
    def _():
        unpack(got_second, True, is_top())
        unpack(got_first, False, False)

    clear_levels(e0)
    clear_levels(e1)
    for k in range(BANDS):
        at = pl.ds(8 * k, 8)
        south, north = corners[0, at, :], corners[1, at, :]
        for f in range(4):
            for side in range(2):
                low, high = turned(pe[f, side, 0, at, :], 24), turned(pe[f, side, 1, at, :], -24)
                total = jnp.where(lane < 64, low, high)
                total = jnp.where(jnp.logical_or(lane < 24, lane >= 104), 0.0, total)
                for g in range(2):
                    n = f * 4 + side * 2 + g
                    total = jnp.where(lane // 8 == 2 - g, turned(south, 8 * (2 - g - n)), total)
                    total = jnp.where(lane // 8 == 13 + g, turned(north, 8 * (13 + g - n)), total)
                if f < 2:
                    e0[f, side, 0, pl.ds(PAD + 8 * k, 8), :] = total
                else:
                    eflow[f - 2, side, 0, at, :] = total
    for side in range(2):
        depths = edge_depths(dp, side, RIM_SOUTH + RIM_NORTH)
        edge_coefs(side, 1, depths, eflow.at[0], eflow.at[1], ecoef, eck, edge_speed)
    edge_beside(1, e0, beside.at[0])
    edge_step(1, e0, e1, ecoef, eck)
    edge_beside(1, e1, beside.at[1])
    edge_step(1, e1, e0, ecoef, eck)
    edge_beside(1, e0, beside.at[2])

    south, north = GHOST, GHOST + ROWS

    for i in [south - 3 + j for j in range(3)] + [north - 1 + j for j in range(3)]:
        make_faces(i, vp, dp, cr, ct)
    for j in range(3):
        a, b = south - 2 + j, north - 1 + j
        for i in (a, b):
            make_column(i, dp, ck)
        make_cells([(a, 0, a), (b, 0, b - north + 13)], up, dp, edge_speed, *coefs)

    for step in range(3):
        old, new = (x, y) if step != 1 else (y, x)
        rows = []
        for j in range(3):
            a, b = south - 2 + step + j, north - 1 - step + j
            rows += [(a, 0, a), (b, 0, b - north + 13)]

        def shift(n, rows=rows, old=old, step=step):
            for k in range(BANDS):
                shift_row(rows[n], k, old, beside.at[step], shifted.at[n])

        shift(0)
        shift(1)
        for n in range(6):
            if n < 4:
                shift(n + 2)
            for k in range(BANDS):
                advance_row(rows[n][0], k, old, new, shifted.at[n], *coefs)
    for start in (south, north - GHOST):
        send_rows([start + n for n in range(3)], y, result, sem)
    sent = y.at[:, pl.ds(0, 2 * GHOST), :, pl.ds(PAD, LEV), :]
    pltpu.make_async_copy(sent, sent, sem).wait()


def shape(*dims):
    return jax.ShapeDtypeStruct(dims, F32)


def vmem(dims):
    return pltpu.VMEM(dims, F32)


def near(*arrays):
    return [pltpu.with_memory_space_constraint(array, pltpu.VMEM) for array in arrays]


def far(*arrays):
    return [pltpu.with_memory_space_constraint(array, pltpu.HBM) for array in arrays]


IN_VMEM = pl.BlockSpec(memory_space=pltpu.VMEM)
IN_HBM = pl.BlockSpec(memory_space=pltpu.HBM)
STATE = (2, PLANES, 2, DEEP, 128)
COEF = (PLANES, 2, LEV, 128)
COLUMN = (PLANES, 2, DEEP, 128)
DEPTH = (3, DROW + ROWS + 8, 128)
SHIFTED = (2, 4, LEV, 128)
EDGES = (4, 2, 2, LEV, 128)


def edge_scratch(parts):
    return [
        vmem((2, 2, parts, DEEP, 128)),
        vmem((2, 2, parts, DEEP, 128)),
        vmem((2, parts, 5, LEV, 128)),
        vmem((2, parts, DEEP, 128)),
        vmem((parts, LEV, 128)),
        vmem((3, 2, parts, LEV, 128)),
    ]


def call(kernel, args, outs, aliases=None, limit=4, **more):
    return pl.pallas_call(
        kernel,
        out_shape=outs,
        input_output_aliases=aliases or {},
        compiler_params=pltpu.CompilerParams(vmem_limit_bytes=limit << 20),
        **more,
    )(*args)


def cost(flops, moved):
    return pl.CostEstimate(flops=flops, bytes_accessed=moved, transcendentals=0)


def local(tracers, u_east, v_north, bottom):
    lon_size, lat_size = lax.axis_size("lon"), lax.axis_size("lat")
    inputs = (*far(tracers, u_east, v_north), bottom)
    x, up, vp, dp, strip = call(
        load_kernel,
        inputs,
        [vmem(STATE), vmem(COEF), vmem(COEF), vmem(DEPTH), shape(STRIP, 128)],
        in_specs=[IN_HBM] * 3 + [IN_VMEM],
        out_specs=[IN_VMEM] * 5,
        scratch_shapes=[pltpu.SemaphoreType.DMA((3,))],
        name="load",
    )
    eastward = [(i, (i + 1) % lon_size) for i in range(lon_size)]
    from_west = lax.ppermute(strip, "lon", eastward)
    from_east = lax.ppermute(strip, "lon", [(b, a) for a, b in eastward])
    first, second = call(
        rows_kernel,
        near(x, up, vp, dp),
        [vmem((PACKED, 128))] * 2,
        in_specs=[IN_VMEM] * 4,
        out_specs=[IN_VMEM] * 2,
        scratch_shapes=[pltpu.SemaphoreType.DMA((2,))],
        name="rows",
        cost_estimate=cost(1_000_000, 4_000_000),
    )
    cr, ct, ck = call(
        faces_kernel,
        near(vp, dp),
        [vmem(COEF), vmem(COEF), vmem(COLUMN)],
        in_specs=[IN_VMEM] * 2,
        out_specs=[IN_VMEM] * 3,
        name="faces",
        cost_estimate=cost(6_000_000, 8_000_000),
    )
    pe, dp, first, second = call(
        corner_kernel,
        (from_east, from_west, strip, *near(dp, first, second)),
        [vmem(EDGES), vmem(DEPTH), vmem((PACKED, 128)), vmem((PACKED, 128))],
        {3: 1, 4: 2, 5: 3},
        in_specs=[IN_VMEM] * 6,
        out_specs=[IN_VMEM] * 4,
        name="corner",
    )
    got_first = lax.ppermute(first, "lat", [(lat, lat ^ 1) for lat in range(lat_size)])
    pairs = []
    for lon in range(lon_size):
        pairs.append((lon * lat_size, (lon ^ 1) * lat_size))
        for lat in range(1, lat_size - 1):
            pairs.append((lon * lat_size + lat, lon * lat_size + (lat + 1 if lat % 2 else lat - 1)))
        pairs.append((lon * lat_size + lat_size - 1, (lon_size - 1 - lon) * lat_size + lat_size - 1))
    got_second = lax.ppermute(second, ("lon", "lat"), pairs)

    x, y, cc, ce, cw, result = call(
        inner_kernel,
        near(x, up, dp, cr, ct, ck, pe),
        [vmem(STATE), vmem(STATE)] + [vmem(COEF)] * 3 + [shape(*tracers.shape)],
        {0: 0},
        limit=16,
        in_specs=[IN_VMEM] * 7,
        out_specs=[IN_VMEM] * 5 + [IN_HBM],
        scratch_shapes=[vmem((2, *SHIFTED)), *edge_scratch(2), pltpu.SemaphoreType.DMA(())],
        name="inner",
        cost_estimate=cost(60_000_000, 20_000_000),
    )
    held = [x, y, cc, ce, cw, cr, ct, ck, up, vp, dp]
    sizes = [STATE, STATE] + [COEF] * 5 + [COLUMN, COEF, COEF, DEPTH]
    edge_lists = edge_scratch(1)
    return call(
        rim_kernel,
        (got_first, got_second, *near(*held, pe), *far(result)),
        [vmem(s) for s in sizes] + [shape(*tracers.shape)],
        {2 + n: n for n in range(11)} | {14: 11},
        limit=16,
        in_specs=[IN_VMEM] * 14 + [IN_HBM],
        out_specs=[IN_VMEM] * 11 + [IN_HBM],
        scratch_shapes=[
            vmem((6, *SHIFTED)), *edge_lists[:2], vmem((2, 2, 1, LEV, 128)), *edge_lists[2:],
            vmem((2, LEV, 128)), pltpu.SemaphoreType.DMA(()),
        ],
        name="rim",
    )[-1]


def solution(mesh):
    placed = (
        P(None, None, "lat", "lon"),
        P(None, "lat", "lon"),
        P(None, "lat", "lon"),
        P("lat", "lon"),
    )
    return jax.shard_map(
        local, mesh=mesh, in_specs=placed, out_specs=P(None, None, "lat", "lon"), check_vma=False
    )
```

```python
import functools

import jax
import jax.numpy as jnp
from jax import lax
from jax.experimental import pallas as pl
from jax.experimental.pallas import tpu as pltpu
from jax.sharding import PartitionSpec as P

LEV = 48
BANDS = LEV // 8
ROWS = 32
COLS = 256
GHOST = 3
PLANES = ROWS + 2 * GHOST
PAD = 8
DEEP = 64
DROW = 8
COPIED = 7
ITEMS = COPIED + 2
DEPTHS = ITEMS * 2 * LEV
CORNERS = DEPTHS + 16
CORNER = LEV + 16
PACKED = CORNERS + CORNER
STRIP = 4 * 2 * LEV
SENT = 4 * LEV + ROWS
H_KAPPA = 0.06
V_KAPPA = 0.08
SHUT = 1e30
F32 = jnp.float32


def lanes():
    return lax.broadcasted_iota(jnp.int32, (8, 128), 1)


def turned(x, shift):
    return pltpu.roll(x, shift % 128 if isinstance(shift, int) else lax.rem(shift + 1024, 128), 1)


def gathered(x, index):
    return jnp.take_along_axis(x, index, axis=1)


def is_top():
    return lax.axis_index("lat") == lax.axis_size("lat") - 1


def is_even():
    return lax.axis_index("lat") % 2 == 0


def mirror(out, n):
    back = 127 - lanes()
    for k in range(BANDS):
        a = pl.ds(2 * n * LEV + 8 * k, 8)
        b = pl.ds((2 * n + 1) * LEV + 8 * k, 8)
        left, right = out[a, :], out[b, :]
        out[a, :] = gathered(right, back)
        out[b, :] = gathered(left, back)


def row_copies(x, up, vp, dp, first, second, sems):
    even = is_even()

    def fill(out, north, sem):
        def row(i):
            return jnp.where(north, ROWS - 1 - i, i) + GHOST

        def face(j):
            return jnp.where(north, ROWS - 1 - j, 0) + GHOST

        items = [(x.at[t], row(i), PAD) for t in range(2) for i in range(2)]
        items += [(vp, face(0), 0), (vp, face(1), 0), (up, row(0), 0)]
        for n, (ref, i, offset) in enumerate(items):
            for half in range(2):
                pltpu.make_async_copy(
                    ref.at[i, half, pl.ds(offset, LEV), :],
                    out.at[pl.ds((2 * n + half) * LEV, LEV), :],
                    sem,
                ).start()

    def finish(out, north, sem):
        all_items = out.at[pl.ds(0, COPIED * 2 * LEV), :]
        pltpu.make_async_copy(all_items, all_items, sem).wait()
        out[pl.ds(DEPTHS, 16), :] = jnp.zeros((16, 128), F32)
        for i in range(3):
            r = jnp.where(north, ROWS - 1 - i, i)
            for half in range(2):
                out[pl.ds(DEPTHS + 2 * i + half, 1), :] = dp[half, pl.ds(r + DROW, 1), :]

    odd = jnp.logical_not(even)
    fill(first, even, sems.at[0])
    fill(second, odd, sems.at[1])
    def end():
        finish(first, even, sems.at[0])
        finish(second, odd, sems.at[1])

        @pl.when(is_top())
        def _():
            back = 127 - lanes()

            def turn(n, _):
                mirror(second, n)
                return 0

            lax.fori_loop(0, COPIED, turn, 0)
            rows = gathered(second[pl.ds(DEPTHS, 8), :], back)
            for i in range(3):
                for half in range(2):
                    source = 2 * i + 1 - half
                    second[pl.ds(DEPTHS + 2 * i + half, 1), :] = rows[source : source + 1, :]

    return end


def load_kernel(tr, u, v, bottom, x, up, vp, dp, strip, to_west, to_east, wet, sems):
    wet_copy = pltpu.make_async_copy(bottom, wet, sems.at[3])
    wet_copy.start()
    for source, into, sem in ((u, up, sems.at[1]), (v, vp, sems.at[2])):
        for r in range(ROWS):
            for half in range(2):
                columns = pl.ds(128 * half, 128)
                pltpu.make_async_copy(source.at[:, r, columns], into.at[r + GHOST, half], sem).start()

    def start_tracers(r):
        for half in range(2):
            pltpu.make_async_copy(
                tr.at[:, :, r, pl.ds(128 * half, 128)],
                x.at[:, r + GHOST, half, pl.ds(PAD, LEV), :],
                sems.at[0],
            ).start()

    wet_copy.wait()
    depth = wet[...].astype(F32)
    dp[...] = jnp.zeros_like(dp)
    for half in range(2):
        dp[half, pl.ds(DROW, ROWS), :] = depth[:, 128 * half : 128 * half + 128]
    strip_lane = lax.broadcasted_iota(jnp.int32, (ROWS, 128), 1)
    edges = jnp.where(strip_lane < 64, depth[:, :128], depth[:, 128:])
    to_west[pl.ds(4 * LEV, ROWS), :] = edges
    to_east[pl.ds(4 * LEV, ROWS), :] = edges

    zeros = jnp.zeros((8, 128), F32)
    lane = lanes()

    def clear(i, _):
        for t in range(2):
            for half in range(2):
                x[t, i, half, pl.ds(0, 8), :] = zeros
                x[t, i, half, pl.ds(DEEP - 8, 8), :] = zeros
        return 0

    lax.fori_loop(0, PLANES, clear, 0)

    def pack(f, load, starting=False):
        def one(j, _):
            for n in range(2):
                k = 2 * j + n
                halves = []
                for part in range(2):
                    total = zeros
                    for s in range(16):
                        if starting and s % 6 == 0:
                            r = (k * 2 + part) * 3 + s // 6
                            if r < ROWS:
                                start_tracers(r)
                        a, b = load(part * 16 + s + GHOST, k)
                        both = turned(jnp.where(lane < 64, a, b), 8 * s + 3)
                        total = jnp.where(lane // 8 == s, both, total)
                    strip[pl.ds((f * 2 + part) * LEV + 8 * k, 8), :] = total
                    halves.append(total)
                at = pl.ds(f * LEV + 8 * k, 8)
                to_west[at, :] = jnp.where(lane % 8 < 3, turned(halves[1], -3), halves[0])
                to_east[at, :] = jnp.where(lane % 8 < 3, halves[0], turned(halves[1], 3))
            return 0

        if starting:
            for r in range(BANDS * 6, ROWS):
                start_tracers(r)
            for j in range(BANDS // 2):
                one(j, 0)
        else:
            lax.fori_loop(0, BANDS // 2, one, 0)

    own = pl.ds(GHOST, ROWS)
    for n, ref in ((1, up), (2, vp)):
        pltpu.make_async_copy(ref.at[own], ref.at[own], sems.at[n]).wait()
        if n == 2:

            @pl.when(is_top())
            def _():
                for half in range(2):
                    vp[GHOST + ROWS - 1, half] = jnp.zeros((LEV, 128), F32)

        pack(n + 1, lambda i, k, ref=ref: [ref[i, half, pl.ds(8 * k, 8), :] for half in range(2)], n == 1)
    whole = x.at[:, own, :, pl.ds(PAD, LEV), :]
    pltpu.make_async_copy(whole, whole, sems.at[0]).wait()
    for t in range(2):
        pack(t, lambda i, k, t=t: [x[t, i, half, pl.ds(PAD + 8 * k, 8), :] for half in range(2)])


def level_of(k):
    return (lax.broadcasted_iota(jnp.int32, (8, 128), 0) + 8 * k).astype(F32)


def above_of(k):
    level = level_of(k)
    return jnp.where(level > 0.0, level, 1e9) if k == 0 else level


def forth(speed, opened):
    return jnp.where(opened, jnp.maximum(speed, 0.0) + H_KAPPA, 0.0)


def back(speed, opened):
    return jnp.where(opened, H_KAPPA - jnp.minimum(speed, 0.0), 0.0)


def depth_row(dp, i, count):
    at = pl.ds(i - GHOST + DROW, 1)
    return [jnp.broadcast_to(dp[n, at, :], (8, 128)) for n in range(count)]


def make_faces(i, vp, dp, cr, ct):
    here, north = depth_row(dp, i, 2), depth_row(dp, i + 1, 2)
    for n in range(2):
        least = jnp.minimum(here[n], north[n])
        for k in range(BANDS):
            at = pl.ds(8 * k, 8)
            speed = vp[i, n, at, :]
            opened = level_of(k) < least
            cr[i, n, at, :] = forth(speed, opened)
            ct[i, n, at, :] = back(speed, opened)


def make_column(i, dp, ck):
    here = depth_row(dp, i, 2)
    for n in range(2):
        ck[i, n, pl.ds(0, 8), :] = jnp.zeros((8, 128), F32)
        for k in range(BANDS):
            ck[i, n, pl.ds(PAD + 8 * k, 8), :] = jnp.where(level_of(k) + 1.0 < here[n], V_KAPPA, 0.0)


def make_cells(rows, up, dp, edge_speed, cc, ce, cw, cr, ct, ck):
    lane = lanes()
    leasts = []
    for i, _, _ in rows:
        here = depth_row(dp, i, 3)
        east = [turned(h, -1) for h in here]
        leasts.append([jnp.minimum(here[n], jnp.where(lane == 127, east[n + 1], east[n])) for n in range(2)])
    for k in range(BANDS):
        at = pl.ds(8 * k, 8)
        for (i, part, slot), least in zip(rows, leasts):
            speeds = [jnp.where(level_of(k) < least[n], up[i, n, at, :], SHUT) for n in range(2)]
            a, b = [turned(speed, 1) for speed in speeds]
            outer = a if edge_speed is None else turned(edge_speed[part, at, :], -8 * slot - 2)
            wests = [jnp.where(lane == 0, outer, a), jnp.where(lane == 0, a, b)]
            for n in range(2):
                open_e, open_w = speeds[n] < SHUT, wests[n] < SHUT
                to_east = forth(speeds[n], open_e)
                from_east = back(speeds[n], open_e)
                ce[i, n, at, :] = from_east
                cw[i, n, at, :] = forth(wests[n], open_w)
                column = ck[i, n, pl.ds(PAD + 8 * k, 8), :] + ck[i, n, pl.ds(PAD + 8 * k - 1, 8), :]
                flows = (to_east + back(wests[n], open_w)) + (cr[i, n, at, :] + ct[i - 1, n, at, :])
                cc[i, n, at, :] = 1.0 - (flows + column)


def next_slot(tiles, lane):
    moved = [turned(t, -8) for t in tiles]
    return [jnp.where(lane >= 120, moved[(p + 1) % len(tiles)], moved[p]) for p in range(len(tiles))]


def last_slot(tiles, lane):
    moved = [turned(t, 8) for t in tiles]
    return [jnp.where(lane < 8, moved[p - 1], moved[p]) for p in range(len(tiles))]


def edge_depths(dp, side, rows):
    lane = lanes()
    tiles = []
    for part in range(len(rows) // 16):
        total = jnp.zeros((8, 128), F32)
        for s in range(16):
            near, beyond = depth_row(dp, rows[part * 16 + s] + GHOST, 3)[side], None
            beyond = depth_row(dp, rows[part * 16 + s] + GHOST, 3)[2]
            both = jnp.where(lane < 64, near, beyond) if side == 0 else jnp.where(lane < 64, beyond, near)
            total = jnp.where(lane // 8 == s, turned(both, 8 * s + 3), total)
        tiles.append(total)
    return tiles


def edge_coefs(side, parts, depths, eu, ev, ecoef, eck, edge_speed):
    lane = lanes()
    depth_e = [turned(d, -1) for d in depths]
    depth_n = next_slot(depths, lane)
    every = range(parts)
    for k in range(BANDS):
        at = pl.ds(8 * k, 8)
        level = level_of(k)
        us = [eu[side, p, at, :] for p in every]
        vs = [ev[side, p, at, :] for p in every]
        open_e = [level < jnp.minimum(depths[p], depth_e[p]) for p in every]
        open_n = [level < jnp.minimum(depths[p], depth_n[p]) for p in every]
        outs = [forth(us[p], open_e[p]) for p in every]
        backs = [back(us[p], open_e[p]) for p in every]
        norths = [forth(vs[p], open_n[p]) for p in every]
        souths = [back(vs[p], open_n[p]) for p in every]
        from_south, to_south = last_slot(norths, lane), last_slot(souths, lane)
        for p in every:
            down = jnp.where(level + 1.0 < depths[p], V_KAPPA, 0.0)
            upward = jnp.where(above_of(k) < depths[p], V_KAPPA, 0.0)
            flows = (outs[p] + turned(backs[p], 1)) + (norths[p] + to_south[p])
            ecoef[side, p, 0, at, :] = 1.0 - (flows + (down + upward))
            ecoef[side, p, 1, at, :] = backs[p]
            ecoef[side, p, 2, at, :] = turned(outs[p], 1)
            ecoef[side, p, 3, at, :] = souths[p]
            ecoef[side, p, 4, at, :] = from_south[p]
            eck[side, p, pl.ds(PAD + 8 * k, 8), :] = down
            if k == 0:
                eck[side, p, pl.ds(0, 8), :] = jnp.zeros((8, 128), F32)
            if side == 0:
                edge_speed[p, at, :] = jnp.where(open_e[p], us[p], SHUT)


def edge_step(parts, old, new, ecoef, eck):
    lane = lanes()

    def one(j, _):
        t = j // 2
        side = j % 2
        for k in range(BANDS):
            at = pl.ds(8 * k, 8)
            here = pl.ds(PAD + 8 * k, 8)
            above = pl.ds(PAD + 8 * k - 1, 8)
            below = pl.ds(PAD + 8 * k + 1, 8)
            tiles = [old[t, side, p, here, :] for p in range(parts)]
            north, south = next_slot(tiles, lane), last_slot(tiles, lane)
            for p in range(parts):
                c = [ecoef[side, p, n, at, :] for n in range(5)]
                total = c[0] * tiles[p] + c[1] * turned(tiles[p], -1) + c[2] * turned(tiles[p], 1)
                total += c[3] * north[p] + c[4] * south[p]
                total += eck[side, p, above, :] * old[t, side, p, above, :]
                total += eck[side, p, here, :] * old[t, side, p, below, :]
                new[t, side, p, here, :] = total
        return 0

    lax.fori_loop(0, 4, one, 0)


def edge_beside(parts, old, beside):
    lane = lanes()
    for t in range(2):
        for p in range(parts):
            for k in range(BANDS):
                here = pl.ds(PAD + 8 * k, 8)
                west, east = old[t, 0, p, here, :], old[t, 1, p, here, :]
                beside[t, p, pl.ds(8 * k, 8), :] = jnp.where(lane % 8 == 3, east, turned(west, 2))


def clear_levels(ref):
    zeros = jnp.zeros((8, 128), F32)
    for t in range(2):
        for side in range(2):
            for p in range(ref.shape[2]):
                ref[t, side, p, pl.ds(0, 8), :] = zeros
                ref[t, side, p, pl.ds(DEEP - 8, 8), :] = zeros


def early_kernel(x, up, vp, dp, cc, ce, cw, cr, ct, ck, beside, first, second, sems):
    end = row_copies(x, up, vp, dp, first, second, sems)
    lane = lanes()

    def one(j, _):
        for n in range(2):
            r = 2 * j + n
            i = r + GHOST
            make_faces(i, vp, dp, cr, ct)
            make_column(i, dp, ck)
            make_cells([(i, 0, 0)], up, dp, None, cc, ce, cw, cr, ct, ck)
            for k in range(BANDS):
                at = pl.ds(8 * k, 8)
                here = pl.ds(PAD + 8 * k, 8)
                for t in range(2):
                    left, right = x[t, i, 0, here, :], x[t, i, 1, here, :]
                    right_e, left_w = turned(right, -1), turned(left, 1)
                    beside[r, t, 0, at, :] = jnp.where(lane == 127, right_e, turned(left, -1))
                    beside[r, t, 1, at, :] = right_e
                    beside[r, t, 2, at, :] = left_w
                    beside[r, t, 3, at, :] = jnp.where(lane == 0, left_w, turned(right, 1))
        return 0

    lax.fori_loop(0, ROWS // 2, one, 0)
    end()


def corner_kernel(
    from_east, from_west, strip, x, ahead, cr, ct, ck, dp_in, first_in, second_in, cc_in, ce_in, cw_in,
    dp, first, second, cc, ce, cw, pe, y, e0, ecoef, eck, patch, beside, edge_speed,
):
    lane = lanes()
    zeros = jnp.zeros((8, 128), F32)
    strip_lane = lax.broadcasted_iota(jnp.int32, (ROWS, 128), 1)
    edge = pl.ds(4 * LEV, ROWS)
    dp[2, pl.ds(DROW, ROWS), :] = jnp.where(strip_lane < 64, from_east[edge, :], from_west[edge, :])
    outer = lane % 8 < 3
    for f in range(4):
        for k in range(BANDS):
            at = pl.ds(f * LEV + 8 * k, 8)
            to = pl.ds(8 * k, 8)
            west, east = from_west[at, :], from_east[at, :]
            for part in range(2):
                mine = strip[pl.ds((f * 2 + part) * LEV + 8 * k, 8), :]
                pe[f, 0, part, to, :] = jnp.where(outer, turned(west, -3) if part else west, mine)
                pe[f, 1, part, to, :] = jnp.where(outer, mine, turned(east, 3) if part else east)

    def fill(out, north):
        part = jnp.where(north, 1, 0)
        for k in range(BANDS):
            total = jnp.zeros((8, 128), F32)
            for f in range(4):
                for side in range(2):
                    tile = pe[f, side, part, pl.ds(8 * k, 8), :]
                    for g in range(2):
                        n = f * 4 + side * 2 + g
                        moved = turned(tile, 8 * jnp.where(north, n - 15 + g, n - g))
                        total = jnp.where(lane // 8 == n, moved, total)
            out[pl.ds(CORNERS + 8 * k, 8), :] = total
        out[pl.ds(CORNERS + LEV, 16), :] = jnp.zeros((16, 128), F32)
        for i in range(3):
            r = jnp.where(north, ROWS - 1 - i, i)
            out[pl.ds(CORNERS + LEV + i, 1), :] = dp[2, pl.ds(r + DROW, 1), :]

    fill(first, is_even())
    fill(second, jnp.logical_not(is_even()))

    def clear(i, _):
        for t in range(2):
            for n in range(2):
                y[t, i, n, pl.ds(0, 8), :] = zeros
                y[t, i, n, pl.ds(DEEP - 8, 8), :] = zeros
        return 0

    lax.fori_loop(0, PLANES, clear, 0)
    clear_levels(e0)
    for side in range(2):
        depths = edge_depths(dp, side, list(range(ROWS)))
        edge_coefs(side, 2, depths, pe.at[2], pe.at[3], ecoef, eck, edge_speed)
        for t in range(2):
            for p in range(2):
                e0[t, side, p, pl.ds(PAD, LEV), :] = pe[t, side, p]
    for p in range(2):
        for k in range(BANDS):
            at = pl.ds(8 * k, 8)
            last = lane % 8 == 2
            patch[0, p, at, :] = jnp.where(last, ecoef[1, p, 0, at, :], ecoef[0, p, 0, at, :])
            patch[1, p, at, :] = jnp.where(last, ecoef[1, p, 1, at, :], ecoef[0, p, 2, at, :])
    edge_beside(2, e0, beside)
    near_south, near_north = GHOST + 1, GHOST + ROWS - 2
    for k in range(BANDS):
        for row in ((near_south, 0, 1), (near_north, 1, 14)):
            first_row(row, k, x, y, ahead, beside, patch, cc, ce, cw, cr, ct, ck)
    for out, north in ((first, is_even()), (second, jnp.logical_not(is_even()))):
        i = jnp.where(north, near_north, near_south)
        for t in range(2):
            for half in range(2):
                at = pl.ds((2 * (COPIED + t) + half) * LEV, LEV)
                out[at, :] = y[t, i, half, pl.ds(PAD, LEV), :]

    @pl.when(is_top())
    def _():
        mirror(second, COPIED)
        mirror(second, COPIED + 1)
        place = lane % 8
        source = jnp.where(lane >= 96, (lane // 8 ^ 2) | 1, lane // 8 ^ 2)
        index = 8 * source + jnp.where(place < 6, 5 - place, place)
        for k in range(BANDS):
            at = pl.ds(CORNERS + 8 * k, 8)
            second[at, :] = gathered(second[at, :], index)
        at = pl.ds(CORNERS + LEV, 8)
        second[at, :] = gathered(second[at, :], 127 - lane)


def shift_row(row, k, old, beside, shifted):
    i, part, slot = row
    lane = lanes()
    here = pl.ds(PAD + 8 * k, 8)
    at = pl.ds(8 * k, 8)
    for t in range(2):
        left, right = old[t, i, 0, here, :], old[t, i, 1, here, :]
        outer = turned(beside[t, part, at, :], -8 * slot - 4)
        left_e, right_e = turned(left, -1), turned(right, -1)
        left_w, right_w = turned(left, 1), turned(right, 1)
        shifted[t, 0, at, :] = jnp.where(lane == 127, right_e, left_e)
        shifted[t, 1, at, :] = jnp.where(lane == 127, outer, right_e)
        shifted[t, 2, at, :] = jnp.where(lane == 0, outer, left_w)
        shifted[t, 3, at, :] = jnp.where(lane == 0, left_w, right_w)


def advance_row(i, k, old, new, shifted, cc, ce, cw, cr, ct, ck):
    at = pl.ds(8 * k, 8)
    here = pl.ds(PAD + 8 * k, 8)
    above = pl.ds(PAD + 8 * k - 1, 8)
    below = pl.ds(PAD + 8 * k + 1, 8)
    for n in range(2):
        c_c, c_e, c_w = cc[i, n, at, :], ce[i, n, at, :], cw[i, n, at, :]
        c_n, c_s = ct[i, n, at, :], cr[i - 1, n, at, :]
        c_d, c_u = ck[i, n, here, :], ck[i, n, above, :]
        for t in range(2):
            total = c_c * old[t, i, n, here, :]
            total += c_e * shifted[t, n, at, :] + c_w * shifted[t, 2 + n, at, :]
            total += c_n * old[t, i + 1, n, here, :] + c_s * old[t, i - 1, n, here, :]
            total += c_u * old[t, i, n, above, :] + c_d * old[t, i, n, below, :]
            new[t, i, n, here, :] = total


def send_rows(rows, new, result, sem):
    for i in rows:
        for half in range(2):
            pltpu.make_async_copy(
                new.at[:, i, half, pl.ds(PAD, LEV), :],
                result.at[:, :, i - GHOST, pl.ds(128 * half, 128)],
                sem,
            ).start()


def first_row(row, k, old, new, ahead, beside, patch, cc, ce, cw, cr, ct, ck):
    i, part, slot = row
    lane = lanes()
    at = pl.ds(8 * k, 8)
    here = pl.ds(PAD + 8 * k, 8)
    above = pl.ds(PAD + 8 * k - 1, 8)
    below = pl.ds(PAD + 8 * k + 1, 8)
    edge = [lane == 0, lane == 127]
    centre = turned(patch[0, part, at, :], -8 * slot - 3)
    sides = turned(patch[1, part, at, :], -8 * slot - 3)
    outer = [turned(beside[t, part, at, :], -8 * slot - 4) for t in range(2)]
    for n in range(2):
        c_c = jnp.where(edge[n], centre, cc[i, n, at, :])
        cc[i, n, at, :] = c_c
        c_e, c_w = ce[i, n, at, :], cw[i, n, at, :]
        if n == 0:
            c_w = jnp.where(edge[0], sides, c_w)
            cw[i, n, at, :] = c_w
        else:
            c_e = jnp.where(edge[1], sides, c_e)
            ce[i, n, at, :] = c_e
        c_n, c_s = ct[i, n, at, :], cr[i - 1, n, at, :]
        c_d, c_u = ck[i, n, here, :], ck[i, n, above, :]
        for t in range(2):
            east, west = ahead[i - GHOST, t, n, at, :], ahead[i - GHOST, t, 2 + n, at, :]
            if n == 0:
                west = jnp.where(edge[0], outer[t], west)
            else:
                east = jnp.where(edge[1], outer[t], east)
            total = c_c * old[t, i, n, here, :] + c_e * east + c_w * west
            total += c_n * old[t, i + 1, n, here, :] + c_s * old[t, i - 1, n, here, :]
            total += c_u * old[t, i, n, above, :] + c_d * old[t, i, n, below, :]
            new[t, i, n, here, :] = total


def inner_kernel(
    x_in, y_in, cc_in, ce_in, cw_in, cr, ct, ck, e0_in, ecoef, eck, patch, ahead, beside_in,
    x, y, cc, ce, cw, result, e0, shifted, e1, beside, sem,
):
    coefs = (cc, ce, cw, cr, ct, ck)

    def placed(i):
        i = jnp.minimum(i, GHOST + ROWS - 1)
        return i, (i - GHOST) // 16, (i - GHOST) % 16

    def first(j, _):
        for n in range(2):
            for k in range(BANDS):
                first_row(placed(GHOST + 2 + 2 * j + n), k, x, y, ahead, beside_in, patch, *coefs)
        return 0

    lax.fori_loop(0, ROWS // 2 - 2, first, 0)
    clear_levels(e1)
    edge_step(2, e0, e1, ecoef, eck)
    edge_beside(2, e1, beside.at[0])
    edge_step(2, e1, e0, ecoef, eck)
    edge_beside(2, e0, beside.at[1])

    for step in range(1, 3):
        old, new = (x, y) if step != 1 else (y, x)
        low = GHOST + 1 + step
        count = ROWS - 2 - 2 * step
        for n in range(2):
            for k in range(BANDS):
                shift_row(placed(low + n), k, old, beside.at[step - 1], shifted.at[n])

        def body(j, _, low=low, old=old, new=new, step=step):
            i = low + 4 * j
            for n in range(4):
                for k in range(BANDS):
                    shift_row(placed(i + n + 2), k, old, beside.at[step - 1], shifted.at[(n + 2) % 4])
                    advance_row(i + n, k, old, new, shifted.at[n], *coefs)
            if step == 2:
                send_rows([i + n for n in range(4)], new, result, sem)
            return 0

        lax.fori_loop(0, count // 4, body, 0)
        for n in range(count % 4):
            i = low + count - count % 4 + n
            for k in range(BANDS):
                advance_row(i, k, old, new, shifted.at[n], *coefs)
            send_rows([i], new, result, sem)
    sent = y.at[:, pl.ds(2 * GHOST, ROWS - 2 * GHOST), :, pl.ds(PAD, LEV), :]
    pltpu.make_async_copy(sent, sent, sem).wait()


RIM_SOUTH = list(range(-GHOST, 5))
RIM_NORTH = list(range(ROWS - 5, ROWS + GHOST))


def rim_kernel(
    got_second, got_first,
    x_in, y_in, cc_in, ce_in, cw_in, cr_in, ct_in, ck_in, up_in, vp_in, dp_in, pe, result_in,
    x, y, cc, ce, cw, cr, ct, ck, up, vp, dp, result,
    shifted, e0, e1, eflow, ecoef, eck, edge_speed, beside, corners, sem,
):
    lane = lanes()
    coefs = (cc, ce, cw, cr, ct, ck)
    bottommost = lax.axis_index("lat") == 0

    def unpack(got, north, mirrored):
        corner = got.at[pl.ds(CORNERS, CORNER), :]

        def plane(i):
            return GHOST + ROWS + i if north else GHOST - 1 - i

        places = [(x.at[t], plane(i), PAD) for t in range(2) for i in range(2)]
        places += [(vp, plane(j - 1 if north else j), 0) for j in range(2)]
        places += [(up, plane(0), 0)] + [(y.at[t], plane(1), PAD) for t in range(2)]
        for n, (ref, i, offset) in enumerate(places):
            if north and n == 4:
                continue
            for k in range(BANDS):
                at = pl.ds(offset + 8 * k, 8)
                tiles = [got[pl.ds((2 * n + half) * LEV + 8 * k, 8), :] for half in range(2)]
                if north and n == 5:
                    tiles = [jnp.where(mirrored, -tile, tile) for tile in tiles]
                if north and n == 6:
                    beyond = turned(corner[pl.ds(8 * k, 8), :], -8 * (2 * 4 + 2) - 3)
                    moved = [turned(tile, -1) for tile in tiles]
                    east = [
                        jnp.where(lane == 127, moved[1], moved[0]),
                        jnp.where(lane == 127, turned(beyond, -1), moved[1]),
                    ]
                    tiles = [jnp.where(mirrored, -b, a) for a, b in zip(tiles, east)]
                for half in range(2):
                    ref[i, half, at, :] = tiles[half]
        for i in range(3):
            at = pl.ds(plane(i) - GHOST + DROW, 1)
            rows = [got[pl.ds(DEPTHS + 2 * i + half, 1), :] for half in range(2)]
            rows.append(corner[pl.ds(LEV + i, 1), :])
            for third in range(3):
                dp[third, at, :] = rows[third] if north else jnp.where(bottommost, 0.0, rows[third])
        for k in range(BANDS):
            at = pl.ds(8 * k, 8)
            tile = corner[at, :]
            if north:
                west_face = -turned(tile, -1)
                changed = jnp.where(lane >= 96, -tile, jnp.where(lane >= 64, west_face, tile))
                tile = jnp.where(mirrored, changed, tile)
            corners[1 if north else 0, at, :] = tile

    @pl.when(is_even())
    def _():
        unpack(got_first, True, False)
        unpack(got_second, False, False)

    @pl.when(jnp.logical_not(is_even()))
    def _():
        unpack(got_second, True, is_top())
        unpack(got_first, False, False)

    clear_levels(e0)
    clear_levels(e1)
    for k in range(BANDS):
        at = pl.ds(8 * k, 8)
        south, north = corners[0, at, :], corners[1, at, :]
        for f in range(4):
            for side in range(2):
                low, high = turned(pe[f, side, 0, at, :], 24), turned(pe[f, side, 1, at, :], -24)
                total = jnp.where(lane < 64, low, high)
                total = jnp.where(jnp.logical_or(lane < 24, lane >= 104), 0.0, total)
                for g in range(2):
                    n = f * 4 + side * 2 + g
                    total = jnp.where(lane // 8 == 2 - g, turned(south, 8 * (2 - g - n)), total)
                    total = jnp.where(lane // 8 == 13 + g, turned(north, 8 * (13 + g - n)), total)
                if f < 2:
                    e0[f, side, 0, pl.ds(PAD + 8 * k, 8), :] = total
                else:
                    eflow[f - 2, side, 0, at, :] = total
    for side in range(2):
        depths = edge_depths(dp, side, RIM_SOUTH + RIM_NORTH)
        edge_coefs(side, 1, depths, eflow.at[0], eflow.at[1], ecoef, eck, edge_speed)
    edge_beside(1, e0, beside.at[0])
    edge_step(1, e0, e1, ecoef, eck)
    edge_beside(1, e1, beside.at[1])
    edge_step(1, e1, e0, ecoef, eck)
    edge_beside(1, e0, beside.at[2])

    south, north = GHOST, GHOST + ROWS

    for i in (south - 2, south - 1, north - 1, north):
        make_faces(i, vp, dp, cr, ct)
    for j in range(2):
        a, b = south - 1 + j, north - 1 + j
        for i in (a, b):
            make_column(i, dp, ck)
        make_cells([(a, 0, a), (b, 0, b - north + 13)], up, dp, edge_speed, *coefs)

    for step in range(3):
        old, new = (x, y) if step != 1 else (y, x)
        rows = []
        for j in range(1 if step == 0 else 0, 3):
            a, b = south - 2 + step + j, north + 1 - step - j
            rows += [(a, 0, a), (b, 0, b - north + 13)]

        def shift(n, rows=rows, old=old, step=step):
            for k in range(BANDS):
                shift_row(rows[n], k, old, beside.at[step], shifted.at[n])

        shift(0)
        shift(1)
        for n in range(len(rows)):
            if n + 2 < len(rows):
                shift(n + 2)
            for k in range(BANDS):
                advance_row(rows[n][0], k, old, new, shifted.at[n], *coefs)
    for start in (south, north - GHOST):
        send_rows([start + n for n in range(3)], y, result, sem)
    sent = y.at[:, pl.ds(0, 2 * GHOST), :, pl.ds(PAD, LEV), :]
    pltpu.make_async_copy(sent, sent, sem).wait()


def shape(*dims):
    return jax.ShapeDtypeStruct(dims, F32)


def vmem(dims):
    return pltpu.VMEM(dims, F32)


def near(*arrays):
    return [pltpu.with_memory_space_constraint(array, pltpu.VMEM) for array in arrays]


def far(*arrays):
    return [pltpu.with_memory_space_constraint(array, pltpu.HBM) for array in arrays]


IN_VMEM = pl.BlockSpec(memory_space=pltpu.VMEM)
IN_HBM = pl.BlockSpec(memory_space=pltpu.HBM)
STATE = (2, PLANES, 2, DEEP, 128)
COEF = (PLANES, 2, LEV, 128)
COLUMN = (PLANES, 2, DEEP, 128)
DEPTH = (3, DROW + ROWS + 8, 128)
SHIFTED = (2, 4, LEV, 128)
AHEAD = (ROWS, *SHIFTED)
EDGES = (4, 2, 2, LEV, 128)


def edge_scratch(parts):
    return [
        vmem((2, 2, parts, DEEP, 128)),
        vmem((2, 2, parts, DEEP, 128)),
        vmem((2, parts, 5, LEV, 128)),
        vmem((2, parts, DEEP, 128)),
        vmem((parts, LEV, 128)),
        vmem((3, 2, parts, LEV, 128)),
    ]


def call(kernel, args, outs, aliases=None, limit=4, **more):
    return pl.pallas_call(
        kernel,
        out_shape=outs,
        input_output_aliases=aliases or {},
        compiler_params=pltpu.CompilerParams(vmem_limit_bytes=limit << 20),
        **more,
    )(*args)


def cost(flops, moved):
    return pl.CostEstimate(flops=flops, bytes_accessed=moved, transcendentals=0)


def local(tracers, u_east, v_north, bottom):
    lon_size, lat_size = lax.axis_size("lon"), lax.axis_size("lat")
    inputs = far(tracers, u_east, v_north, bottom)
    x, up, vp, dp, strip, to_west, to_east = call(
        load_kernel,
        inputs,
        [vmem(d) for d in [STATE, COEF, COEF, DEPTH, (STRIP, 128)]] + [shape(SENT, 128)] * 2,
        in_specs=[IN_HBM] * 4,
        out_specs=[IN_VMEM] * 7,
        scratch_shapes=[pltpu.VMEM((ROWS, COLS), jnp.int32), pltpu.SemaphoreType.DMA((4,))],
        name="load",
    )
    eastward = [(i, (i + 1) % lon_size) for i in range(lon_size)]
    from_west = lax.ppermute(to_east, "lon", eastward)
    from_east = lax.ppermute(to_west, "lon", [(b, a) for a, b in eastward])
    cc, ce, cw, cr, ct, ck, ahead, first, second = call(
        early_kernel,
        near(x, up, vp, dp),
        [vmem(COEF)] * 5 + [vmem(COLUMN), vmem(AHEAD), vmem((PACKED, 128)), vmem((PACKED, 128))],
        in_specs=[IN_VMEM] * 4,
        out_specs=[IN_VMEM] * 9,
        scratch_shapes=[pltpu.SemaphoreType.DMA((2,))],
        name="early",
        cost_estimate=cost(12_000_000, 14_000_000),
    )
    dp, first, second, cc, ce, cw, pe, y, e0, ecoef, eck, patch, beside = call(
        corner_kernel,
        (from_east, from_west, *near(strip, x, ahead, cr, ct, ck, dp, first, second, cc, ce, cw)),
        [vmem(d) for d in [DEPTH, (PACKED, 128), (PACKED, 128)] + [COEF] * 3 + [EDGES, STATE]]
        + [*edge_scratch(2)[1:4], vmem((2, 2, LEV, 128)), vmem((2, 2, LEV, 128))],
        {8: 0, 9: 1, 10: 2, 11: 3, 12: 4, 13: 5},
        in_specs=[IN_VMEM] * 14,
        out_specs=[IN_VMEM] * 13,
        scratch_shapes=[vmem((2, LEV, 128))],
        name="corner",
    )
    pairs = []
    for lon in range(lon_size):
        pairs.append((lon * lat_size, (lon ^ 1) * lat_size))
        for lat in range(1, lat_size - 1):
            pairs.append((lon * lat_size + lat, lon * lat_size + (lat + 1 if lat % 2 else lat - 1)))
        pairs.append((lon * lat_size + lat_size - 1, (lon_size - 1 - lon) * lat_size + lat_size - 1))
    got_second = lax.ppermute(second, ("lon", "lat"), pairs)
    got_first = lax.ppermute(first, "lat", [(lat, lat ^ 1) for lat in range(lat_size)])

    x, y, cc, ce, cw, result, _ = call(
        inner_kernel,
        near(x, y, cc, ce, cw, cr, ct, ck, e0, ecoef, eck, patch, ahead, beside),
        [vmem(STATE), vmem(STATE)] + [vmem(COEF)] * 3 + [shape(*tracers.shape), edge_scratch(2)[0]],
        {0: 0, 1: 1, 2: 2, 3: 3, 4: 4, 8: 6},
        limit=12,
        in_specs=[IN_VMEM] * 14,
        out_specs=[IN_VMEM] * 5 + [IN_HBM, IN_VMEM],
        scratch_shapes=[
            vmem((4, *SHIFTED)), edge_scratch(2)[0], vmem((2, 2, 2, LEV, 128)), pltpu.SemaphoreType.DMA(()),
        ],
        name="inner",
        cost_estimate=cost(60_000_000, 20_000_000),
    )
    held = [x, y, cc, ce, cw, cr, ct, ck, up, vp, dp]
    sizes = [STATE, STATE] + [COEF] * 5 + [COLUMN, COEF, COEF, DEPTH]
    edge_lists = edge_scratch(1)
    return call(
        rim_kernel,
        (got_second, got_first, *near(*held, pe), *far(result)),
        [vmem(s) for s in sizes] + [shape(*tracers.shape)],
        {2 + n: n for n in range(11)} | {14: 11},
        limit=16,
        in_specs=[IN_VMEM] * 14 + [IN_HBM],
        out_specs=[IN_VMEM] * 11 + [IN_HBM],
        scratch_shapes=[
            vmem((6, *SHIFTED)), *edge_lists[:2], vmem((2, 2, 1, LEV, 128)), *edge_lists[2:],
            vmem((2, LEV, 128)), pltpu.SemaphoreType.DMA(()),
        ],
        name="rim",
    )[-1]


def solution(mesh):
    placed = (
        P(None, None, "lat", "lon"),
        P(None, "lat", "lon"),
        P(None, "lat", "lon"),
        P("lat", "lon"),
    )
    return jax.shard_map(
        local, mesh=mesh, in_specs=placed, out_specs=P(None, None, "lat", "lon"), check_vma=False
    )
```

```python
import functools

import jax
import jax.numpy as jnp
from jax import lax
from jax.experimental import pallas as pl
from jax.experimental.pallas import tpu as pltpu
from jax.sharding import PartitionSpec as P

LEV = 48
BANDS = LEV // 8
ROWS = 32
COLS = 256
GHOST = 3
PLANES = ROWS + 2 * GHOST
PAD = 8
DEEP = 64
NEAR = (GHOST + 1, GHOST + ROWS - 2)
DROW = 8
COPIED = 7
ITEMS = COPIED + 2
DEPTHS = ITEMS * 2 * LEV
CORNERS = DEPTHS + 16
CORNER = LEV + 16
PACKED = CORNERS + CORNER
STRIP = 4 * 2 * LEV
SENT = 4 * LEV + ROWS
H_KAPPA = 0.06
V_KAPPA = 0.08
SHUT = 1e30
F32 = jnp.float32


def lanes():
    return lax.broadcasted_iota(jnp.int32, (8, 128), 1)


def turned(x, shift):
    return pltpu.roll(x, shift % 128 if isinstance(shift, int) else lax.rem(shift + 1024, 128), 1)


def gathered(x, index):
    return jnp.take_along_axis(x, index, axis=1)


def lane_tile(n):
    return pl.ds(128 * n, 128)


def is_top():
    return lax.axis_index("lat") == lax.axis_size("lat") - 1


def is_even():
    return lax.axis_index("lat") % 2 == 0


def mirror(out, n):
    back = 127 - lanes()
    for k in range(BANDS):
        a = pl.ds(2 * n * LEV + 8 * k, 8)
        b = pl.ds((2 * n + 1) * LEV + 8 * k, 8)
        left, right = out[a, :], out[b, :]
        out[a, :] = gathered(right, back)
        out[b, :] = gathered(left, back)


def row_copies(x, up, vp, dp, first, second, sems):
    even = is_even()

    def fill(out, north, sem):
        def row(i):
            return jnp.where(north, ROWS - 1 - i, i) + GHOST

        def face(j):
            return jnp.where(north, ROWS - 1 - j, 0) + GHOST

        items = [(x.at[t], row(i)) for t in range(2) for i in range(2)]
        items += [(vp, face(0)), (vp, face(1)), (up, row(0))]
        for n, (ref, i) in enumerate(items):
            for half in range(2):
                pltpu.make_async_copy(
                    ref.at[i, half, pl.ds(PAD, LEV), :] if n < 4 else ref.at[i, :, lane_tile(half)],
                    out.at[pl.ds((2 * n + half) * LEV, LEV), :],
                    sem,
                ).start()

    def finish(out, north, sem):
        all_items = out.at[pl.ds(0, COPIED * 2 * LEV), :]
        pltpu.make_async_copy(all_items, all_items, sem).wait()
        out[pl.ds(DEPTHS, 16), :] = jnp.zeros((16, 128), F32)
        for i in range(3):
            r = jnp.where(north, ROWS - 1 - i, i)
            for half in range(2):
                out[pl.ds(DEPTHS + 2 * i + half, 1), :] = dp[half, pl.ds(r + DROW, 1), :]

    odd = jnp.logical_not(even)
    fill(first, even, sems.at[0])
    fill(second, odd, sems.at[1])
    def end():
        finish(first, even, sems.at[0])
        finish(second, odd, sems.at[1])

        @pl.when(is_top())
        def _():
            back = 127 - lanes()

            def turn(n, _):
                mirror(second, n)
                return 0

            lax.fori_loop(0, COPIED, turn, 0)
            rows = gathered(second[pl.ds(DEPTHS, 8), :], back)
            for i in range(3):
                for half in range(2):
                    source = 2 * i + 1 - half
                    second[pl.ds(DEPTHS + 2 * i + half, 1), :] = rows[source : source + 1, :]

    return end


def load_kernel(tr, u, v, bottom, x, up, vp, dp, strip, to_west, to_east, wet, sems):
    wet_copy = pltpu.make_async_copy(bottom, wet, sems.at[3])
    wet_copy.start()
    for source, into, sem in ((u, up, sems.at[1]), (v, vp, sems.at[2])):
        for r in range(ROWS):
            pltpu.make_async_copy(source.at[:, r, :], into.at[r + GHOST], sem).start()

    def start_tracers(r):
        for half in range(2):
            pltpu.make_async_copy(
                tr.at[:, :, r, pl.ds(128 * half, 128)],
                x.at[:, r + GHOST, half, pl.ds(PAD, LEV), :],
                sems.at[0],
            ).start()

    wet_copy.wait()
    depth = wet[...].astype(F32)
    dp[...] = jnp.zeros_like(dp)
    for half in range(2):
        dp[half, pl.ds(DROW, ROWS), :] = depth[:, 128 * half : 128 * half + 128]
    strip_lane = lax.broadcasted_iota(jnp.int32, (ROWS, 128), 1)
    edges = jnp.where(strip_lane < 64, depth[:, :128], depth[:, 128:])
    to_west[pl.ds(4 * LEV, ROWS), :] = edges
    to_east[pl.ds(4 * LEV, ROWS), :] = edges

    zeros = jnp.zeros((8, 128), F32)
    lane = lanes()

    def clear(i, _):
        for t in range(2):
            for half in range(2):
                x[t, i, half, pl.ds(0, 8), :] = zeros
                x[t, i, half, pl.ds(DEEP - 8, 8), :] = zeros
        return 0

    lax.fori_loop(0, PLANES, clear, 0)

    def pack(f, load, starting=False):
        def one(j, _):
            for n in range(2):
                k = 2 * j + n
                halves = []
                for part in range(2):
                    total = zeros
                    for s in range(16):
                        if starting and s % 6 == 0:
                            r = (k * 2 + part) * 3 + s // 6
                            if r < ROWS:
                                start_tracers(r)
                        a, b = load(part * 16 + s + GHOST, k)
                        both = turned(jnp.where(lane < 64, a, b), 8 * s + 3)
                        total = jnp.where(lane // 8 == s, both, total)
                    strip[pl.ds((f * 2 + part) * LEV + 8 * k, 8), :] = total
                    halves.append(total)
                at = pl.ds(f * LEV + 8 * k, 8)
                to_west[at, :] = jnp.where(lane % 8 < 3, turned(halves[1], -3), halves[0])
                to_east[at, :] = jnp.where(lane % 8 < 3, halves[0], turned(halves[1], 3))
            return 0

        if starting:
            for r in range(BANDS * 6, ROWS):
                start_tracers(r)
            for j in range(BANDS // 2):
                one(j, 0)
        else:
            lax.fori_loop(0, BANDS // 2, one, 0)

    own = pl.ds(GHOST, ROWS)
    for n, ref in ((1, up), (2, vp)):
        pltpu.make_async_copy(ref.at[own], ref.at[own], sems.at[n]).wait()
        if n == 2:

            @pl.when(is_top())
            def _():
                vp[GHOST + ROWS - 1] = jnp.zeros((LEV, COLS), F32)

        pack(n + 1, lambda i, k, ref=ref: [ref[i, pl.ds(8 * k, 8), lane_tile(half)] for half in range(2)], n == 1)
    whole = x.at[:, own, :, pl.ds(PAD, LEV), :]
    pltpu.make_async_copy(whole, whole, sems.at[0]).wait()
    for t in range(2):
        pack(t, lambda i, k, t=t: [x[t, i, half, pl.ds(PAD + 8 * k, 8), :] for half in range(2)])


def level_of(k):
    return (lax.broadcasted_iota(jnp.int32, (8, 128), 0) + 8 * k).astype(F32)


def above_of(k):
    level = level_of(k)
    return jnp.where(level > 0.0, level, 1e9) if k == 0 else level


def forth(speed, opened):
    return jnp.where(opened, jnp.maximum(speed, 0.0) + H_KAPPA, 0.0)


def back(speed, opened):
    return jnp.where(opened, H_KAPPA - jnp.minimum(speed, 0.0), 0.0)


def depth_row(dp, i, count):
    at = pl.ds(i - GHOST + DROW, 1)
    return [jnp.broadcast_to(dp[n, at, :], (8, 128)) for n in range(count)]


def make_faces(i, vp, dp, cr, ct):
    here, north = depth_row(dp, i, 2), depth_row(dp, i + 1, 2)
    for n in range(2):
        least = jnp.minimum(here[n], north[n])
        for k in range(BANDS):
            at = pl.ds(8 * k, 8)
            speed = vp[i, at, lane_tile(n)]
            opened = level_of(k) < least
            cr[i, n, at, :] = forth(speed, opened)
            ct[i, n, at, :] = back(speed, opened)


def make_column(i, dp, ck):
    here = depth_row(dp, i, 2)
    for n in range(2):
        ck[i, n, pl.ds(0, 8), :] = jnp.zeros((8, 128), F32)
        for k in range(BANDS):
            ck[i, n, pl.ds(PAD + 8 * k, 8), :] = jnp.where(level_of(k) + 1.0 < here[n], V_KAPPA, 0.0)


def make_cells(rows, up, dp, edge_speed, cc, ce, cw, cr, ct, ck):
    lane = lanes()
    leasts = []
    for i, _, _ in rows:
        here = depth_row(dp, i, 3)
        east = [turned(h, -1) for h in here]
        leasts.append([jnp.minimum(here[n], jnp.where(lane == 127, east[n + 1], east[n])) for n in range(2)])
    for k in range(BANDS):
        at = pl.ds(8 * k, 8)
        for (i, part, slot), least in zip(rows, leasts):
            speeds = [jnp.where(level_of(k) < least[n], up[i, at, lane_tile(n)], SHUT) for n in range(2)]
            a, b = [turned(speed, 1) for speed in speeds]
            outer = a if edge_speed is None else turned(edge_speed[part, at, :], -8 * slot - 2)
            wests = [jnp.where(lane == 0, outer, a), jnp.where(lane == 0, a, b)]
            for n in range(2):
                open_e, open_w = speeds[n] < SHUT, wests[n] < SHUT
                to_east = forth(speeds[n], open_e)
                from_east = back(speeds[n], open_e)
                ce[i, n, at, :] = from_east
                cw[i, n, at, :] = forth(wests[n], open_w)
                column = ck[i, n, pl.ds(PAD + 8 * k, 8), :] + ck[i, n, pl.ds(PAD + 8 * k - 1, 8), :]
                flows = (to_east + back(wests[n], open_w)) + (cr[i, n, at, :] + ct[i - 1, n, at, :])
                cc[i, n, at, :] = 1.0 - (flows + column)


def next_slot(tiles, lane):
    moved = [turned(t, -8) for t in tiles]
    return [jnp.where(lane >= 120, moved[(p + 1) % len(tiles)], moved[p]) for p in range(len(tiles))]


def last_slot(tiles, lane):
    moved = [turned(t, 8) for t in tiles]
    return [jnp.where(lane < 8, moved[p - 1], moved[p]) for p in range(len(tiles))]


def edge_depths(dp, side, rows):
    lane = lanes()
    tiles = []
    for part in range(len(rows) // 16):
        total = jnp.zeros((8, 128), F32)
        for s in range(16):
            near, beyond = depth_row(dp, rows[part * 16 + s] + GHOST, 3)[side], None
            beyond = depth_row(dp, rows[part * 16 + s] + GHOST, 3)[2]
            both = jnp.where(lane < 64, near, beyond) if side == 0 else jnp.where(lane < 64, beyond, near)
            total = jnp.where(lane // 8 == s, turned(both, 8 * s + 3), total)
        tiles.append(total)
    return tiles


def edge_coefs(side, parts, depths, eu, ev, ecoef, eck, edge_speed):
    lane = lanes()
    depth_e = [turned(d, -1) for d in depths]
    depth_n = next_slot(depths, lane)
    if parts == 2:
        depth_n[1] = jnp.where(lane >= 120, 0.0, depth_n[1])
    every = range(parts)
    for k in range(BANDS):
        at = pl.ds(8 * k, 8)
        level = level_of(k)
        us = [eu[side, p, at, :] for p in every]
        vs = [ev[side, p, at, :] for p in every]
        open_e = [level < jnp.minimum(depths[p], depth_e[p]) for p in every]
        open_n = [level < jnp.minimum(depths[p], depth_n[p]) for p in every]
        outs = [forth(us[p], open_e[p]) for p in every]
        backs = [back(us[p], open_e[p]) for p in every]
        norths = [forth(vs[p], open_n[p]) for p in every]
        souths = [back(vs[p], open_n[p]) for p in every]
        from_south, to_south = last_slot(norths, lane), last_slot(souths, lane)
        for p in every:
            down = jnp.where(level + 1.0 < depths[p], V_KAPPA, 0.0)
            upward = jnp.where(above_of(k) < depths[p], V_KAPPA, 0.0)
            flows = (outs[p] + turned(backs[p], 1)) + (norths[p] + to_south[p])
            ecoef[side, p, 0, at, :] = 1.0 - (flows + (down + upward))
            ecoef[side, p, 1, at, :] = backs[p]
            ecoef[side, p, 2, at, :] = turned(outs[p], 1)
            ecoef[side, p, 3, at, :] = souths[p]
            ecoef[side, p, 4, at, :] = from_south[p]
            eck[side, p, pl.ds(PAD + 8 * k, 8), :] = down
            if k == 0:
                eck[side, p, pl.ds(0, 8), :] = jnp.zeros((8, 128), F32)
            if side == 0:
                edge_speed[p, at, :] = jnp.where(open_e[p], us[p], SHUT)


def edge_step(parts, old, new, ecoef, eck):
    lane = lanes()

    def one(j, _):
        t = j // 2
        side = j % 2
        for k in range(BANDS):
            at = pl.ds(8 * k, 8)
            here = pl.ds(PAD + 8 * k, 8)
            above = pl.ds(PAD + 8 * k - 1, 8)
            below = pl.ds(PAD + 8 * k + 1, 8)
            tiles = [old[t, side, p, here, :] for p in range(parts)]
            north, south = next_slot(tiles, lane), last_slot(tiles, lane)
            for p in range(parts):
                c = [ecoef[side, p, n, at, :] for n in range(5)]
                total = c[0] * tiles[p] + c[1] * turned(tiles[p], -1) + c[2] * turned(tiles[p], 1)
                total += c[3] * north[p] + c[4] * south[p]
                total += eck[side, p, above, :] * old[t, side, p, above, :]
                total += eck[side, p, here, :] * old[t, side, p, below, :]
                new[t, side, p, here, :] = total
        return 0

    lax.fori_loop(0, 4, one, 0)


def edge_beside(parts, old, beside):
    lane = lanes()
    for t in range(2):
        for p in range(parts):
            for k in range(BANDS):
                here = pl.ds(PAD + 8 * k, 8)
                west, east = old[t, 0, p, here, :], old[t, 1, p, here, :]
                beside[t, p, pl.ds(8 * k, 8), :] = jnp.where(lane % 8 == 3, east, turned(west, 2))


def clear_levels(ref):
    zeros = jnp.zeros((8, 128), F32)
    for t in range(2):
        for side in range(2):
            for p in range(ref.shape[2]):
                ref[t, side, p, pl.ds(0, 8), :] = zeros
                ref[t, side, p, pl.ds(DEEP - 8, 8), :] = zeros


def early_kernel(x, up, vp, dp, cc, ce, cw, cr, ct, ck, beside, first, second, sems):
    end = row_copies(x, up, vp, dp, first, second, sems)
    lane = lanes()
    ct[GHOST - 1] = jnp.zeros((2, LEV, 128), F32)

    def one(j, _):
        for n in range(2):
            r = 2 * j + n
            i = r + GHOST
            make_faces(i, vp, dp, cr, ct)
            make_column(i, dp, ck)
            make_cells([(i, 0, 0)], up, dp, None, cc, ce, cw, cr, ct, ck)
        return 0

    lax.fori_loop(0, ROWS // 2, one, 0)
    for n, i in enumerate(NEAR):
        for k in range(BANDS):
            at = pl.ds(8 * k, 8)
            here = pl.ds(PAD + 8 * k, 8)
            for t in range(2):
                left, right = x[t, i, 0, here, :], x[t, i, 1, here, :]
                right_e, left_w = turned(right, -1), turned(left, 1)
                beside[n, t, 0, at, :] = jnp.where(lane == 127, right_e, turned(left, -1))
                beside[n, t, 1, at, :] = right_e
                beside[n, t, 2, at, :] = left_w
                beside[n, t, 3, at, :] = jnp.where(lane == 0, left_w, turned(right, 1))
    end()


def corner_kernel(
    from_west, from_east, strip, x, ahead, cr, ct, ck, dp_in, first_in, second_in, cc_in, ce_in, cw_in,
    dp, first, second, cc, ce, cw, pe, y, e0, ecoef, eck, patch, beside, edge_speed,
):
    lane = lanes()
    zeros = jnp.zeros((8, 128), F32)
    strip_lane = lax.broadcasted_iota(jnp.int32, (ROWS, 128), 1)
    edge = pl.ds(4 * LEV, ROWS)
    dp[2, pl.ds(DROW, ROWS), :] = jnp.where(strip_lane < 64, from_east[edge, :], from_west[edge, :])
    outer = lane % 8 < 3
    for f in range(4):
        for k in range(BANDS):
            at = pl.ds(f * LEV + 8 * k, 8)
            to = pl.ds(8 * k, 8)
            west, east = from_west[at, :], from_east[at, :]
            for part in range(2):
                mine = strip[pl.ds((f * 2 + part) * LEV + 8 * k, 8), :]
                pe[f, 0, part, to, :] = jnp.where(outer, turned(west, -3) if part else west, mine)
                pe[f, 1, part, to, :] = jnp.where(outer, mine, turned(east, 3) if part else east)

    def fill(out, north):
        part = jnp.where(north, 1, 0)
        for k in range(BANDS):
            total = jnp.zeros((8, 128), F32)
            for f in range(4):
                for side in range(2):
                    tile = pe[f, side, part, pl.ds(8 * k, 8), :]
                    for g in range(2):
                        n = f * 4 + side * 2 + g
                        moved = turned(tile, 8 * jnp.where(north, n - 15 + g, n - g))
                        total = jnp.where(lane // 8 == n, moved, total)
            out[pl.ds(CORNERS + 8 * k, 8), :] = total
        out[pl.ds(CORNERS + LEV, 16), :] = jnp.zeros((16, 128), F32)
        for i in range(3):
            r = jnp.where(north, ROWS - 1 - i, i)
            out[pl.ds(CORNERS + LEV + i, 1), :] = dp[2, pl.ds(r + DROW, 1), :]

    fill(first, is_even())
    fill(second, jnp.logical_not(is_even()))

    def clear(i, _):
        for t in range(2):
            for n in range(2):
                y[t, i, n, pl.ds(0, 8), :] = zeros
                y[t, i, n, pl.ds(DEEP - 8, 8), :] = zeros
        return 0

    lax.fori_loop(0, PLANES, clear, 0)
    clear_levels(e0)
    for side in range(2):
        depths = edge_depths(dp, side, list(range(ROWS)))
        edge_coefs(side, 2, depths, pe.at[2], pe.at[3], ecoef, eck, edge_speed)
        for t in range(2):
            for p in range(2):
                e0[t, side, p, pl.ds(PAD, LEV), :] = pe[t, side, p]
    for p in range(2):
        for k in range(BANDS):
            at = pl.ds(8 * k, 8)
            last = lane % 8 == 2
            patch[0, p, at, :] = jnp.where(last, ecoef[1, p, 0, at, :], ecoef[0, p, 0, at, :])
            patch[1, p, at, :] = jnp.where(last, ecoef[1, p, 1, at, :], ecoef[0, p, 2, at, :])
    edge_beside(2, e0, beside)
    for k in range(BANDS):
        for n, row in enumerate(((NEAR[0], 0, 1), (NEAR[1], 1, 14))):
            first_row(row, k, x, y, ahead.at[n], beside, patch, cc, ce, cw, cr, ct, ck)
    for out, north in ((first, is_even()), (second, jnp.logical_not(is_even()))):
        i = jnp.where(north, NEAR[1], NEAR[0])
        for t in range(2):
            for half in range(2):
                at = pl.ds((2 * (COPIED + t) + half) * LEV, LEV)
                out[at, :] = y[t, i, half, pl.ds(PAD, LEV), :]

    @pl.when(is_top())
    def _():
        mirror(second, COPIED)
        mirror(second, COPIED + 1)
        place = lane % 8
        source = jnp.where(lane >= 96, (lane // 8 ^ 2) | 1, lane // 8 ^ 2)
        index = 8 * source + jnp.where(place < 6, 5 - place, place)
        for k in range(BANDS):
            at = pl.ds(CORNERS + 8 * k, 8)
            second[at, :] = gathered(second[at, :], index)
        at = pl.ds(CORNERS + LEV, 8)
        second[at, :] = gathered(second[at, :], 127 - lane)


def shift_row(row, k, old, beside, shifted):
    i, part, slot = row
    lane = lanes()
    here = pl.ds(PAD + 8 * k, 8)
    at = pl.ds(8 * k, 8)
    for t in range(2):
        left, right = old[t, i, 0, here, :], old[t, i, 1, here, :]
        outer = turned(beside[t, part, at, :], -8 * slot - 4)
        left_e, right_e = turned(left, -1), turned(right, -1)
        left_w, right_w = turned(left, 1), turned(right, 1)
        shifted[t, 0, at, :] = jnp.where(lane == 127, right_e, left_e)
        shifted[t, 1, at, :] = jnp.where(lane == 127, outer, right_e)
        shifted[t, 2, at, :] = jnp.where(lane == 0, outer, left_w)
        shifted[t, 3, at, :] = jnp.where(lane == 0, left_w, right_w)


def advance_row(i, k, old, put, shifted, cc, ce, cw, cr, ct, ck, without=None):
    at = pl.ds(8 * k, 8)
    here = pl.ds(PAD + 8 * k, 8)
    above = pl.ds(PAD + 8 * k - 1, 8)
    below = pl.ds(PAD + 8 * k + 1, 8)
    for n in range(2):
        c_c, c_e, c_w = cc[i, n, at, :], ce[i, n, at, :], cw[i, n, at, :]
        c_n, c_s = ct[i, n, at, :], cr[i - 1, n, at, :]
        c_d, c_u = ck[i, n, here, :], ck[i, n, above, :]
        for t in range(2):
            total = c_c * old[t, i, n, here, :]
            total += c_e * shifted[t, n, at, :] + c_w * shifted[t, 2 + n, at, :]
            if without != "north":
                total += c_n * old[t, i + 1, n, here, :]
            if without != "south":
                total += c_s * old[t, i - 1, n, here, :]
            total += c_u * old[t, i, n, above, :] + c_d * old[t, i, n, below, :]
            put[t, n, pl.ds(put.shape[2] - LEV - PAD * (put.shape[2] > LEV) + 8 * k, 8), :] = total


def send_row(row, r, result, sem):
    for half in range(2):
        pltpu.make_async_copy(
            row.at[:, half], result.at[:, :, r, pl.ds(128 * half, 128)], sem
        ).start()


def patch_row(row, k, patch, cc, ce, cw):
    i, part, slot = row
    lane = lanes()
    at = pl.ds(8 * k, 8)
    centre = turned(patch[0, part, at, :], -8 * slot - 3)
    sides = turned(patch[1, part, at, :], -8 * slot - 3)
    cc[i, 0, at, :] = jnp.where(lane == 0, centre, cc[i, 0, at, :])
    cc[i, 1, at, :] = jnp.where(lane == 127, centre, cc[i, 1, at, :])
    cw[i, 0, at, :] = jnp.where(lane == 0, sides, cw[i, 0, at, :])
    ce[i, 1, at, :] = jnp.where(lane == 127, sides, ce[i, 1, at, :])


def first_row(row, k, old, new, shifted, beside, patch, cc, ce, cw, cr, ct, ck):
    i, part, slot = row
    lane = lanes()
    at = pl.ds(8 * k, 8)
    here = pl.ds(PAD + 8 * k, 8)
    above = pl.ds(PAD + 8 * k - 1, 8)
    below = pl.ds(PAD + 8 * k + 1, 8)
    edge = [lane == 0, lane == 127]
    centre = turned(patch[0, part, at, :], -8 * slot - 3)
    sides = turned(patch[1, part, at, :], -8 * slot - 3)
    if beside is not None:
        outer = [turned(beside[t, part, at, :], -8 * slot - 4) for t in range(2)]
    for n in range(2):
        c_c = jnp.where(edge[n], centre, cc[i, n, at, :])
        cc[i, n, at, :] = c_c
        c_e, c_w = ce[i, n, at, :], cw[i, n, at, :]
        if n == 0:
            c_w = jnp.where(edge[0], sides, c_w)
            cw[i, n, at, :] = c_w
        else:
            c_e = jnp.where(edge[1], sides, c_e)
            ce[i, n, at, :] = c_e
        c_n, c_s = ct[i, n, at, :], cr[i - 1, n, at, :]
        c_d, c_u = ck[i, n, here, :], ck[i, n, above, :]
        for t in range(2):
            east, west = shifted[t, n, at, :], shifted[t, 2 + n, at, :]
            if beside is None:
                pass
            elif n == 0:
                west = jnp.where(edge[0], outer[t], west)
            else:
                east = jnp.where(edge[1], outer[t], east)
            total = c_c * old[t, i, n, here, :] + c_e * east + c_w * west
            total += c_n * old[t, i + 1, n, here, :] + c_s * old[t, i - 1, n, here, :]
            total += c_u * old[t, i, n, above, :] + c_d * old[t, i, n, below, :]
            new[t, i, n, here, :] = total


def inner_kernel(
    x_in, y_in, cc_in, ce_in, cw_in, cr, ct, ck, e0_in, ecoef, eck, patch, beside_in,
    x, y, cc, ce, cw, result, e0, partial, shifted, e1, beside, sem,
):
    coefs = (cc, ce, cw, cr, ct, ck)

    def part_of_rows(step, old, beyond):
        for n, r in enumerate((step, ROWS - 1 - step)):
            row = (r + GHOST, r // 16, r % 16)
            for k in range(BANDS):
                shift_row(row, k, old, beyond, shifted.at[n])
        for n, r in enumerate((step, ROWS - 1 - step)):
            for k in range(BANDS):
                if step == 0:
                    patch_row((r + GHOST, r // 16, r % 16), k, patch, cc, ce, cw)
                put, without = partial.at[step, n], "north" if n else "south"
                advance_row(r + GHOST, k, old, put, shifted.at[n], *coefs, without)

    part_of_rows(0, x, beside_in)

    def placed(i):
        i = jnp.minimum(i, GHOST + ROWS - 1)
        return i, (i - GHOST) // 16, (i - GHOST) % 16

    for n in range(2):
        for k in range(BANDS):
            shift_row(placed(GHOST + 2 + n), k, x, beside_in, shifted.at[n])

    def first(j, _):
        for n in range(RING):
            i = GHOST + 2 + RING * j + n
            for k in range(BANDS):
                shift_row(placed(i + 2), k, x, beside_in, shifted.at[(n + 2) % RING])
                first_row(placed(i), k, x, y, shifted.at[n], None, patch, *coefs)
        return 0

    lax.fori_loop(0, (ROWS - 4) // RING, first, 0)
    clear_levels(e1)
    edge_step(2, e0, e1, ecoef, eck)
    edge_beside(2, e1, beside.at[0])
    edge_step(2, e1, e0, ecoef, eck)
    edge_beside(2, e0, beside.at[1])
    part_of_rows(1, y, beside.at[0])

    for n in range(2):
        for k in range(BANDS):
            shift_row(placed(GHOST + 2 + n), k, y, beside.at[0], shifted.at[n])

    def second(j, _):
        for n in range(RING):
            i = GHOST + 2 + RING * j + n
            for k in range(BANDS):
                shift_row(placed(i + 2), k, y, beside.at[0], shifted.at[(n + 2) % RING])
                advance_row(i, k, y, x.at[:, i], shifted.at[n], *coefs)
        return 0

    lax.fori_loop(0, (ROWS - 4) // RING, second, 0)

    part_of_rows(2, x, beside.at[1])
    for n in range(2):
        for k in range(BANDS):
            shift_row(placed(2 * GHOST + n), k, x, beside.at[1], shifted.at[n])

    def third(j, _):
        for n in range(GROUP):
            i = 2 * GHOST + GROUP * j + n
            for k in range(BANDS):
                shift_row(placed(i + 2), k, x, beside.at[1], shifted.at[(n + 2) % GROUP])
                advance_row(i, k, x, y.at[:, i], shifted.at[n], *coefs)
        for n in range(GROUP):
            i = 2 * GHOST + GROUP * j + n
            send_row(y.at[:, i, :, pl.ds(PAD, LEV), :], i - GHOST, result, sem)
        return 0

    lax.fori_loop(0, (ROWS - 2 * GHOST) // GROUP, third, 0)
    sent = y.at[:, pl.ds(2 * GHOST, ROWS - 2 * GHOST), :, pl.ds(PAD, LEV), :]
    pltpu.make_async_copy(sent, sent, sem).wait()


RIM_SOUTH = list(range(-GHOST, 5))
RIM_NORTH = list(range(ROWS - 5, ROWS + GHOST))


def rim_kernel(
    got_second, got_first,
    x_in, y_in, cc_in, ce_in, cw_in, cr_in, ct_in, ck_in, up_in, vp_in, dp_in, pe, partial, result_in,
    x, y, cc, ce, cw, cr, ct, ck, up, vp, dp, result,
    shifted, e0, e1, eflow, ecoef, eck, edge_speed, beside, corners, sem, *outs,
):
    lane = lanes()
    coefs = (cc, ce, cw, cr, ct, ck)
    bottommost = lax.axis_index("lat") == 0

    def unpack(got, north, mirrored):
        corner = got.at[pl.ds(CORNERS, CORNER), :]

        def plane(i):
            return GHOST + ROWS + i if north else GHOST - 1 - i

        places = [(x.at[t], plane(i), PAD) for t in range(2) for i in range(2)]
        places += [(vp, plane(j - 1 if north else j), 0) for j in range(2)]
        places += [(up, plane(0), 0)] + [(y.at[t], plane(1), PAD) for t in range(2)]
        for n, (ref, i, offset) in enumerate(places):
            if north and n == 4:
                continue
            for k in range(BANDS):
                at = pl.ds(offset + 8 * k, 8)
                tiles = [got[pl.ds((2 * n + half) * LEV + 8 * k, 8), :] for half in range(2)]
                if north and n == 5:
                    tiles = [jnp.where(mirrored, -tile, tile) for tile in tiles]
                if north and n == 6:
                    beyond = turned(corner[pl.ds(8 * k, 8), :], -8 * (2 * 4 + 2) - 3)
                    moved = [turned(tile, -1) for tile in tiles]
                    east = [
                        jnp.where(lane == 127, moved[1], moved[0]),
                        jnp.where(lane == 127, turned(beyond, -1), moved[1]),
                    ]
                    tiles = [jnp.where(mirrored, -b, a) for a, b in zip(tiles, east)]
                for half in range(2):
                    if 4 <= n < 7:
                        ref[i, at, lane_tile(half)] = tiles[half]
                    else:
                        ref[i, half, at, :] = tiles[half]
        for i in range(3):
            at = pl.ds(plane(i) - GHOST + DROW, 1)
            rows = [got[pl.ds(DEPTHS + 2 * i + half, 1), :] for half in range(2)]
            rows.append(corner[pl.ds(LEV + i, 1), :])
            for third in range(3):
                dp[third, at, :] = rows[third] if north else jnp.where(bottommost, 0.0, rows[third])
        for k in range(BANDS):
            at = pl.ds(8 * k, 8)
            tile = corner[at, :]
            if north:
                west_face = -turned(tile, -1)
                changed = jnp.where(lane >= 96, -tile, jnp.where(lane >= 64, west_face, tile))
                tile = jnp.where(mirrored, changed, tile)
            corners[1 if north else 0, at, :] = tile

    @pl.when(is_even())
    def _():
        unpack(got_first, True, False)
        unpack(got_second, False, False)

    @pl.when(jnp.logical_not(is_even()))
    def _():
        unpack(got_second, True, is_top())
        unpack(got_first, False, False)

    clear_levels(e0)
    clear_levels(e1)
    for k in range(BANDS):
        at = pl.ds(8 * k, 8)
        south, north = corners[0, at, :], corners[1, at, :]
        for f in range(4):
            for side in range(2):
                low, high = turned(pe[f, side, 0, at, :], 24), turned(pe[f, side, 1, at, :], -24)
                total = jnp.where(lane < 64, low, high)
                total = jnp.where(jnp.logical_or(lane < 24, lane >= 104), 0.0, total)
                for g in range(2):
                    n = f * 4 + side * 2 + g
                    total = jnp.where(lane // 8 == 2 - g, turned(south, 8 * (2 - g - n)), total)
                    total = jnp.where(lane // 8 == 13 + g, turned(north, 8 * (13 + g - n)), total)
                if f < 2:
                    e0[f, side, 0, pl.ds(PAD + 8 * k, 8), :] = total
                else:
                    eflow[f - 2, side, 0, at, :] = total
    for side in range(2):
        depths = edge_depths(dp, side, RIM_SOUTH + RIM_NORTH)
        edge_coefs(side, 1, depths, eflow.at[0], eflow.at[1], ecoef, eck, edge_speed)
    edge_beside(1, e0, beside.at[0])
    edge_step(1, e0, e1, ecoef, eck)
    edge_beside(1, e1, beside.at[1])
    edge_step(1, e1, e0, ecoef, eck)
    edge_beside(1, e0, beside.at[2])

    south, north = GHOST, GHOST + ROWS

    for i in (south - 2, south - 1, north - 1, north):
        make_faces(i, vp, dp, cr, ct)
    for i in (south - 1, north):
        make_column(i, dp, ck)
    make_cells([(south - 1, 0, south - 1), (north, 0, 13)], up, dp, edge_speed, *coefs)
    for n in range(2):
        for k in range(BANDS):
            at = pl.ds(8 * k, 8)
            cc[south, n, at, :] = cc[south, n, at, :] - ct[south - 1, n, at, :]
            cc[north - 1, n, at, :] = cc[north - 1, n, at, :] - cr[north - 1, n, at, :]

    def complete(i, old, put, share, from_south, step):
        for n in range(2):
            for k in range(BANDS):
                at = pl.ds(8 * k, 8)
                here = pl.ds(PAD + 8 * k, 8)
                inward = cr[i - 1, n, at, :] if from_south else ct[i, n, at, :]
                outward = ct[i - 1, n, at, :] if from_south else cr[i, n, at, :]
                for t in range(2):
                    beyond = old[t, i - 1 if from_south else i + 1, n, here, :]
                    total = share[t, n, at, :] + inward * beyond
                    if step == 0:
                        total -= outward * old[t, i, n, here, :]
                    put[t, n, pl.ds(put.shape[2] - LEV - PAD * (put.shape[2] > LEV) + 8 * k, 8), :] = total

    for step in range(3):
        old, new = (x, y) if step != 1 else (y, x)
        rows = [(south - 1, north), (south - 1, north, south, north - 1), (south, north - 1, south + 1, north - 2)][step]

        def shift(n, rows=rows, old=old, step=step):
            i = rows[n]
            row = (i, 0, i if i < 16 else i - north + 13)
            for k in range(BANDS):
                shift_row(row, k, old, beside.at[step], shifted.at[n])

        shift(0)
        shift(1)
        for n, i in enumerate((south + step, north - 1 - step)):
            put = outs[n] if step == 2 else new.at[:, i]
            complete(i, old, put, partial.at[step, n], n == 0, step)
        if step == 2:
            send_row(outs[0], 2, result, sem)
            send_row(outs[1], ROWS - 3, result, sem)
        for n, i in enumerate(rows):
            if n + 2 < len(rows):
                shift(n + 2)
            for k in range(BANDS):
                put = outs[2 + n] if step == 2 else new.at[:, i]
                advance_row(i, k, old, put, shifted.at[n], *coefs)
            if step == 2 and n:
                send_row(outs[1 + n], rows[n - 1] - GHOST, result, sem)
    send_row(outs[5], rows[3] - GHOST, result, sem)
    for out in outs:
        pltpu.make_async_copy(out, out, sem).wait()


def shape(*dims):
    return jax.ShapeDtypeStruct(dims, F32)


def vmem(dims):
    return pltpu.VMEM(dims, F32)


def near(*arrays):
    return [pltpu.with_memory_space_constraint(array, pltpu.VMEM) for array in arrays]


def far(*arrays):
    return [pltpu.with_memory_space_constraint(array, pltpu.HBM) for array in arrays]


IN_VMEM = pl.BlockSpec(memory_space=pltpu.VMEM)
IN_HBM = pl.BlockSpec(memory_space=pltpu.HBM)
STATE = (2, PLANES, 2, DEEP, 128)
COEF = (PLANES, 2, LEV, 128)
FLOW = (PLANES, LEV, COLS)
COLUMN = (PLANES, 2, DEEP, 128)
DEPTH = (3, DROW + ROWS + 8, 128)
SHIFTED = (2, 4, LEV, 128)
RING = 14
GROUP = 13
AHEAD = (2, *SHIFTED)
EDGES = (4, 2, 2, LEV, 128)


def edge_scratch(parts):
    return [
        vmem((2, 2, parts, DEEP, 128)),
        vmem((2, 2, parts, DEEP, 128)),
        vmem((2, parts, 5, LEV, 128)),
        vmem((2, parts, DEEP, 128)),
        vmem((parts, LEV, 128)),
        vmem((3, 2, parts, LEV, 128)),
    ]


def call(kernel, args, outs, aliases=None, limit=4, **more):
    return pl.pallas_call(
        kernel,
        out_shape=outs,
        input_output_aliases=aliases or {},
        compiler_params=pltpu.CompilerParams(vmem_limit_bytes=limit << 20),
        **more,
    )(*args)


def cost(flops, moved):
    return pl.CostEstimate(flops=flops, bytes_accessed=moved, transcendentals=0)


def local(tracers, u_east, v_north, bottom):
    lon_size, lat_size = lax.axis_size("lon"), lax.axis_size("lat")
    inputs = far(tracers, u_east, v_north, bottom)
    x, up, vp, dp, strip, to_west, to_east = call(
        load_kernel,
        inputs,
        [vmem(d) for d in [STATE, FLOW, FLOW, DEPTH, (STRIP, 128)]] + [shape(SENT, 128)] * 2,
        in_specs=[IN_HBM] * 4,
        out_specs=[IN_VMEM] * 7,
        scratch_shapes=[pltpu.VMEM((ROWS, COLS), jnp.int32), pltpu.SemaphoreType.DMA((4,))],
        name="load",
    )
    eastward = [(i, (i + 1) % lon_size) for i in range(lon_size)]
    from_west = lax.ppermute(to_east, "lon", eastward)
    from_east = lax.ppermute(to_west, "lon", [(b, a) for a, b in eastward])
    cc, ce, cw, cr, ct, ck, ahead, first, second = call(
        early_kernel,
        near(x, up, vp, dp),
        [vmem(COEF)] * 5 + [vmem(COLUMN), vmem(AHEAD), vmem((PACKED, 128)), vmem((PACKED, 128))],
        in_specs=[IN_VMEM] * 4,
        out_specs=[IN_VMEM] * 9,
        scratch_shapes=[pltpu.SemaphoreType.DMA((2,))],
        name="early",
        cost_estimate=cost(12_000_000, 14_000_000),
    )
    dp, first, second, cc, ce, cw, pe, y, e0, ecoef, eck, patch, beside = call(
        corner_kernel,
        (from_west, from_east, *near(strip, x, ahead, cr, ct, ck, dp, first, second, cc, ce, cw)),
        [vmem(d) for d in [DEPTH, (PACKED, 128), (PACKED, 128)] + [COEF] * 3 + [EDGES, STATE]]
        + [*edge_scratch(2)[1:4], vmem((2, 2, LEV, 128)), vmem((2, 2, LEV, 128))],
        {8: 0, 9: 1, 10: 2, 11: 3, 12: 4, 13: 5},
        in_specs=[IN_VMEM] * 14,
        out_specs=[IN_VMEM] * 13,
        scratch_shapes=[vmem((2, LEV, 128))],
        name="corner",
    )
    pairs = []
    for lon in range(lon_size):
        pairs.append((lon * lat_size, (lon ^ 1) * lat_size))
        for lat in range(1, lat_size - 1):
            pairs.append((lon * lat_size + lat, lon * lat_size + (lat + 1 if lat % 2 else lat - 1)))
        pairs.append((lon * lat_size + lat_size - 1, (lon_size - 1 - lon) * lat_size + lat_size - 1))
    got_second = lax.ppermute(second, ("lon", "lat"), pairs)
    got_first = lax.ppermute(first, "lat", [(lat, lat ^ 1) for lat in range(lat_size)])

    x, y, cc, ce, cw, result, _, partial = call(
        inner_kernel,
        near(x, y, cc, ce, cw, cr, ct, ck, e0, ecoef, eck, patch, beside),
        [vmem(STATE), vmem(STATE)] + [vmem(COEF)] * 3 + [shape(*tracers.shape), edge_scratch(2)[0], vmem((3, 2, 2, 2, LEV, 128))],
        {0: 0, 1: 1, 2: 2, 3: 3, 4: 4, 8: 6},
        limit=12,
        in_specs=[IN_VMEM] * 13,
        out_specs=[IN_VMEM] * 5 + [IN_HBM, IN_VMEM, IN_VMEM],
        scratch_shapes=[
            vmem((RING, *SHIFTED)), edge_scratch(2)[0], vmem((2, 2, 2, LEV, 128)), pltpu.SemaphoreType.DMA(()),
        ],
        name="inner",
        cost_estimate=cost(60_000_000, 20_000_000),
    )
    held = [x, y, cc, ce, cw, cr, ct, ck, up, vp, dp]
    sizes = [STATE, STATE] + [COEF] * 5 + [COLUMN, FLOW, FLOW, DEPTH]
    edge_lists = edge_scratch(1)
    return call(
        rim_kernel,
        (got_second, got_first, *near(*held, pe, partial), *far(result)),
        [vmem(s) for s in sizes] + [shape(*tracers.shape)],
        {2 + n: n for n in range(11)} | {15: 11},
        limit=16,
        in_specs=[IN_VMEM] * 15 + [IN_HBM],
        out_specs=[IN_VMEM] * 11 + [IN_HBM],
        scratch_shapes=[
            vmem((6, *SHIFTED)), *edge_lists[:2], vmem((2, 2, 1, LEV, 128)), *edge_lists[2:],
            vmem((2, LEV, 128)), pltpu.SemaphoreType.DMA(()), *[vmem((2, 2, LEV, 128))] * 6,
        ],
        name="rim",
    )[-1]


def solution(mesh):
    placed = (
        P(None, None, "lat", "lon"),
        P(None, "lat", "lon"),
        P(None, "lat", "lon"),
        P("lat", "lon"),
    )
    return jax.shard_map(
        local, mesh=mesh, in_specs=placed, out_specs=P(None, None, "lat", "lon"), check_vma=False
    )
```
